32 devices in a mesh: shard: 4 (over x, core), rep: 8 (over z, y).
Axes of the slice: x: 2, y: 2, z: 4, core: 2. Of those that a mesh axis runs over, the one named last changes fastest.
Arguments:
- grads: bfloat16 [4, 8, 262144], P('shard', 'rep'), may hold values from -5000 to 5000
- momentum_codes: int32 [262144], P(('shard', 'rep')), may hold values from -127 to 127
- variance_codes: int32 [262144], P(('shard', 'rep')), may hold values from 16 to 255
- momentum_scale: float32 [160], P(('shard', 'rep')), may hold values from 0.5 to 4, as said below
- variance_scale: float32 [160], P(('shard', 'rep')), may hold values from 1 to 4, as said below
- master: float32 [262144], P(('shard', 'rep')), may hold values from -2.5 to 2.5
- step: int32 [1], replicated, may hold values from 1 to 19
Outputs:
- new_master: float32 [262144], P(('shard', 'rep'))
- weights: bfloat16 [262144], P('shard')
- update: float32 [262144], P(('shard', 'rep'))
- momentum_norm: float32 [262144], P(('shard', 'rep'))
- variance_norm: float32 [262144], P(('shard', 'rep'))
- momentum_absmax: float32 [160], P(('shard', 'rep'))
- variance_absmax: float32 [160], P(('shard', 'rep'))
The draws below stay inside these ranges and needn't reach their ends.
Inputs may be any that keep to these rules, and one draw needn't show every extreme that they name: `momentum_scale`: A block touched by two neighbouring devices has the same value in both devices' slots. `variance_scale`: A block touched by two neighbouring devices has the same value in both devices' slots.
All inputs are finite; a program needn't handle non-finite values.
Results may differ from the reference program's by a relative error of at most 0.0004.
Values may be sent and summed in bfloat16 or wider, within the bound.
No kernel may reach another device: no remote copies, remote signals or barrier semaphores. Data moves between devices by JAX's collectives and lax.ppermute only.
A program may use at most 64 MiB of HBM per device.

```python
import math
import jax
import jax.numpy as jnp
from jax import lax

BLOCK = 2048
FULL_BLOCKS = 4
OWN = 8192
SLOTS = 5
PARAMS = 262144
N_SHARD = 4
N_REP = 8
DEVICES = 32


def slot_blocks():
    owner = jnp.arange(DEVICES, dtype=jnp.int32)[:, None]
    slot = jnp.arange(SLOTS, dtype=jnp.int32)[None, :]
    return (owner * FULL_BLOCKS + slot).reshape(-1).astype(jnp.int32)


def draw_scale(key, low, high):
    nblocks = PARAMS // BLOCK + 1
    values = jnp.exp(jax.random.uniform(key, (nblocks,), jnp.float32, math.log(low), math.log(high)))
    return values[slot_blocks()]


def draw_momentum_scale(key, part):
    return draw_scale(jax.random.fold_in(key, 11), 0.5, 4.0)


def draw_variance_scale(key, part):
    return draw_scale(jax.random.fold_in(key, 23), 1.0, 4.0)


def plant_codes(key, low, high, peak, upper, signed):
    nblocks = PARAMS // BLOCK + 1
    half_len = BLOCK // 2
    key_base, key_place, key_sign = jax.random.split(key, 3)
    base = jax.random.randint(key_base, (PARAMS,), low, high, dtype=jnp.int32)
    entry = jnp.arange(PARAMS, dtype=jnp.int32)
    block = (entry + half_len) // BLOCK
    within = (entry + half_len) % BLOCK
    place = jax.random.randint(key_place, (nblocks,), 0, half_len, dtype=jnp.int32)
    if upper:
        place = place + half_len
    chosen = within == place[block]
    if signed:
        signs = jax.random.randint(key_sign, (nblocks,), 0, 2, dtype=jnp.int32) * 2 - 1
        signs = signs.at[0].set(1).at[1].set(-1)
        planted = peak * signs[block]
    else:
        planted = jnp.full((PARAMS,), peak, jnp.int32)
    return jnp.where(chosen, planted, base).astype(jnp.int32)


def draw_momentum_codes(key, part):
    return plant_codes(jax.random.fold_in(key, 41), -63, 64, 127, True, True)


def draw_variance_codes(key, part):
    return plant_codes(jax.random.fold_in(key, 43), 16, 129, 255, False, False)


def draw_grads(key, part):
    keys = jax.random.split(jax.random.fold_in(key, 37), 9)
    nblocks = PARAMS // BLOCK
    position = jnp.arange(PARAMS, dtype=jnp.float32) / float(PARAMS)
    roughness = jnp.repeat(jnp.exp(jax.random.uniform(keys[0], (nblocks,), jnp.float32, 0.0, math.log(10.0))), BLOCK)
    device_scale = jnp.exp(jax.random.uniform(keys[1], (N_SHARD, N_REP, 1), jnp.float32, 0.0, math.log(3.0)))
    noise = jnp.clip(jax.random.normal(keys[2], (N_SHARD, N_REP, PARAMS), jnp.float32), -4.0, 4.0)
    perm_a = jax.random.permutation(keys[3], N_SHARD).astype(jnp.int32)
    perm_b = jax.random.permutation(keys[4], N_REP).astype(jnp.int32)
    partner = perm_a[:, None] * N_REP + perm_b[None, :]
    owner = jnp.arange(PARAMS, dtype=jnp.int32) // OWN
    heavy = (owner[None, None, :] == partner[:, :, None]).astype(jnp.float32)
    spike = 1.0 + 11.0 * heavy
    trend = jnp.power(3.0, position) * roughness
    quarter = BLOCK // 4
    odd_step = 2 * jax.random.randint(keys[6], (nblocks,), 0, max(quarter // 2, 1), dtype=jnp.int32) + 1
    region = jax.random.randint(keys[7], (nblocks,), 0, 2, dtype=jnp.int32)
    offset = quarter + region * 2 * quarter + odd_step
    sign_flip = (jax.random.randint(keys[8], (nblocks,), 0, 2, dtype=jnp.int32) * 2 - 1).astype(jnp.float32)
    entry = jnp.arange(PARAMS, dtype=jnp.int32)
    group_of = entry // BLOCK
    within = entry % BLOCK
    planted = (within == offset[group_of]).astype(jnp.float32) * sign_flip[group_of]
    spread_sq = 3.64 * float(DEVICES + 143)
    values = noise * device_scale * spike * trend
    height = math.sqrt(float(BLOCK) * spread_sq) / float(DEVICES)
    values = values + (height * planted * trend)[None, None, :]
    return values.astype(jnp.bfloat16)


def level_of(stream_key, extent, pieces, low, top_value):
    def one(axis_at, blocks):
        heights = jax.random.uniform(jax.random.fold_in(jax.random.fold_in(stream_key, 6), axis_at), (blocks,), jnp.float32, low / len(pieces), top_value / len(pieces))
        return jnp.repeat(jnp.exp(heights), extent[axis_at] // blocks).reshape((-1,) + (1,) * (len(extent) - axis_at - 1))

    gain = one(*pieces[0])
    for cut in pieces[1:]:
        gain = gain * one(*cut)
    return gain


def gaussian(key, shape, deviation, reach, cuts=(), kind=jnp.bfloat16):
    array = deviation * jax.random.normal(key, shape, jnp.float32)
    if cuts:
        array = array * level_of(key, shape, cuts, -0.22, 0.18)
    return jnp.clip(array, -reach, reach).astype(kind)


def setup_inputs(seed: int = 0) -> dict:
    key_of = jax.random.split(jax.random.key(seed), 8)
    grads = draw_grads(jax.random.fold_in(key_of[7], 71), 0)
    momentum_codes = draw_momentum_codes(jax.random.fold_in(key_of[7], 71), 0)
    variance_codes = draw_variance_codes(jax.random.fold_in(key_of[7], 71), 0)
    momentum_scale = draw_momentum_scale(jax.random.fold_in(key_of[7], 71), 0)
    variance_scale = draw_variance_scale(jax.random.fold_in(key_of[7], 71), 0)
    master = gaussian(key_of[5], (PARAMS,), 0.5, 2.5, ((0, 32),), jnp.float32)
    step = jax.random.randint(key_of[6], (1,), 1, 20).astype(jnp.int32)
    return {"grads": grads, "momentum_codes": momentum_codes, "variance_codes": variance_codes, "momentum_scale": momentum_scale, "variance_scale": variance_scale, "master": master, "step": step}


def slot_index():
    entry = jnp.arange(PARAMS, dtype=jnp.int32)
    owner = entry // OWN
    local = entry % OWN
    slot = (local + BLOCK // 2) // BLOCK
    return (owner * SLOTS + slot).astype(jnp.int32)

def block_of_slot():
    owner = jnp.arange(DEVICES, dtype=jnp.int32)[:, None]
    slot = jnp.arange(SLOTS, dtype=jnp.int32)[None, :]
    return (owner * FULL_BLOCKS + slot).reshape(-1).astype(jnp.int32)

def reference(grads, momentum_codes, variance_codes, momentum_scale, variance_scale, master, step):
    half = BLOCK // 2
    gsum = lax.optimization_barrier(jnp.sum(grads.astype(jnp.float32), axis=(0, 1)))
    norm_sq = jnp.sum(gsum * gsum)
    clip_factor = jnp.minimum(1.0, float(PARAMS) ** 0.5 / (jnp.sqrt(norm_sq) + 1e-06))
    scaled = gsum * clip_factor
    index = slot_index()
    m_old = momentum_codes.astype(jnp.float32) / 127.0 * momentum_scale[index]
    v_old = variance_codes.astype(jnp.float32) / 255.0 * variance_scale[index]
    momentum = 0.9 * m_old + 0.1 * scaled
    variance = 0.95 * v_old + 0.05 * scaled * scaled
    count = step[0].astype(jnp.float32)
    first_fix = 1.0 - jnp.power(jnp.float32(0.9), count)
    second_fix = 1.0 - jnp.power(jnp.float32(0.95), count)
    update = momentum / first_fix / (jnp.sqrt(variance / second_fix) + 1e-08)
    new_master = master * (1.0 - 0.0001 * 0.1) - 0.0001 * update
    weights = new_master.astype(jnp.bfloat16)
    nblocks = PARAMS // BLOCK + 1
    m_pad = jnp.pad(jnp.abs(momentum), (half, half))
    v_pad = jnp.pad(jnp.abs(variance), (half, half))
    m_block = lax.optimization_barrier(jnp.max(m_pad.reshape(nblocks, BLOCK), axis=1))
    v_block = lax.optimization_barrier(jnp.max(v_pad.reshape(nblocks, BLOCK), axis=1))
    m_elem = jnp.repeat(m_block, BLOCK)[half:half + PARAMS]
    v_elem = jnp.repeat(v_block, BLOCK)[half:half + PARAMS]
    momentum_norm = momentum / (m_elem + 1e-06)
    variance_norm = variance / (v_elem + 1e-06)
    slots = block_of_slot()
    return (new_master, weights, update, momentum_norm, variance_norm, m_block[slots], v_block[slots])
```

```python
import functools

import jax
import jax.numpy as jnp
from jax import lax
from jax.experimental import pallas as pl
from jax.experimental.pallas import tpu as pltpu
from jax.sharding import PartitionSpec as P

BLOCK = 2048
LANES = 128
EDGE = BLOCK // 2 // LANES
ALL = ("shard", "rep")
BF16 = jnp.bfloat16
F32 = jnp.float32
VMEM = pl.BlockSpec(memory_space=pltpu.VMEM)
SMEM = pl.BlockSpec(memory_space=pltpu.SMEM)
ANY = pl.BlockSpec(memory_space=pl.ANY)


class Plan:
    def __init__(self, own_len):
        self.shards = lax.axis_size("shard")
        self.reps = lax.axis_size("rep")
        self.devices = self.shards * self.reps
        self.xs = self.shards // 2
        self.zs = self.reps // 2
        self.groups = self.xs * 2
        self.rows = own_len // LANES

    def swap(self, value, core=0, z=0, group=0):
        x, y = group >> 1, group & 1
        mask = ((x << 1) | core) * self.reps + ((z << 1) | y)
        return lax.ppermute(value, ALL, [(i, i ^ mask) for i in range(self.devices)])


def place():
    shard, rep = lax.axis_index("shard"), lax.axis_index("rep")
    return shard // 2, shard % 2, rep // 2, rep % 2


def tree(values):
    values = list(values)
    while len(values) > 1:
        values = [a + b for a, b in zip(values[::2], values[1::2])]
    return values[0]


def call(kernel, outs, ins, in_specs=None, out_specs=None, scratch=(), limit=16):
    return pl.pallas_call(
        kernel,
        out_shape=outs,
        in_specs=in_specs or [VMEM] * len(ins),
        out_specs=out_specs or jax.tree.map(lambda _: VMEM, outs),
        scratch_shapes=list(scratch),
        compiler_params=pltpu.CompilerParams(vmem_limit_bytes=limit * 1024 * 1024),
    )(*ins)


def half_kernel(flip, count, length, x_ref, o_ref, buf, sem):
    _, core, _, _ = place()
    want = (core + flip) % 2
    rows = length // LANES
    copies = []
    for k in range(count):
        start = pl.multiple_of((2 * k + want) * length, length)
        copies.append(pltpu.make_async_copy(x_ref.at[:, pl.ds(start, length)], buf.at[k], sem.at[k]))
        copies[-1].start()
    for k in range(count):
        copies[k].wait()
        o_ref[pl.ds(k * rows, rows), :] = buf[k].astype(F32).reshape(rows, LANES).astype(BF16)


def half(plan, grads, flip):
    length = plan.reps * plan.rows * LANES
    return call(
        functools.partial(half_kernel, flip, plan.xs, length),
        jax.ShapeDtypeStruct((plan.xs * length // LANES, LANES), BF16),
        [grads],
        in_specs=[ANY],
        scratch=[pltpu.VMEM((plan.xs, 1, length), BF16), pltpu.SemaphoreType.DMA((plan.xs,))],
    )


def pair_kernel(plan, mine_ref, other_ref, *outs):
    x, _, _, y = place()
    for k, out in enumerate(outs):
        to_x, to_y = x ^ (k >> 1), y ^ (k & 1)
        for z in range(plan.zs):
            start = pl.multiple_of((to_x * plan.reps + 2 * z + to_y) * plan.rows, plan.rows)
            rows = pl.ds(start, plan.rows)
            out[pl.ds(z * plan.rows, plan.rows), :] = mine_ref[rows, :].astype(F32) + other_ref[rows, :].astype(F32)


def sum_kernel(*refs):
    refs[-1][...] = tree([r[...] for r in refs[:-1]])


def state_kernel(plan, mc_ref, vc_ref, ms_ref, vs_ref, master_ref, o_ref):
    slots = ms_ref.shape[0]
    for j in range(slots):
        low, high = max(0, (2 * j - 1) * EDGE), min(plan.rows, (2 * j + 1) * EDGE)
        o_ref[low:high, :] = mc_ref[low:high, :].astype(F32) / 127.0 * ms_ref[j]
        o_ref[plan.rows + low : plan.rows + high, :] = vc_ref[low:high, :].astype(F32) / 255.0 * vs_ref[j]
    o_ref[2 * plan.rows :, :] = master_ref[...]


def order_kernel(plan, *refs):
    _, _, z, _ = place()
    for k, ref in enumerate(refs[:-1]):
        refs[-1][z ^ k] = ref[...]


def total_kernel(plan, *refs):
    parts, (state_ref, sum_ref, send_ref) = refs[: plan.zs], refs[plan.zs :]
    _, _, _, y = place()
    total = tree([r[...] for r in parts])
    sum_ref[...] = total
    send_ref[0:8, :] = jnp.sum((total * total).reshape(-1, 8, LANES), axis=0)

    def edge(z, start):
        send_ref[8 : 8 + EDGE, :] = sum_ref[z * plan.rows + start : z * plan.rows + start + EDGE, :]
        for k in range(2):
            at = k * plan.rows + start
            send_ref[8 + (k + 1) * EDGE : 8 + (k + 2) * EDGE, :] = state_ref[z, at : at + EDGE, :]

    @pl.when(y == 0)
    def _():
        edge(0, 0)

    @pl.when(y == 1)
    def _():
        edge(plan.zs - 1, plan.rows - EDGE)


def core_kernel(mine_ref, other_ref, norm_ref, relay_ref):
    norm = mine_ref[0:8, :] + other_ref[0:8, :]
    norm_ref[...] = norm
    relay_ref[0:8, :] = norm
    relay_ref[8:, :] = other_ref[8:, :]


def main_kernel(plan, total_params, *refs):
    norms, refs = refs[: plan.groups], refs[plan.groups :]
    (sum_mine, sum_other, state_mine, state_other, fix_ref) = refs[:5]
    (master_out, weights_out, update_out, mn_out, vn_out, mt_out, vt_out) = refs[5:12]
    m_buf, v_buf, far = refs[12:]
    x, core, z, y = place()
    rows = plan.rows
    slots = mt_out.shape[0]
    norm_sq = jnp.sum(tree([r[0:8, :] for r in norms]), keepdims=True)
    clip = jnp.minimum(1.0, float(total_params) ** 0.5 / (jnp.sqrt(norm_sq) + 1e-06))
    first_fix, second_fix = fix_ref[0], fix_ref[1]

    def moments(grad, m_old, v_old):
        scaled = grad * clip
        return 0.9 * m_old + 0.1 * scaled, 0.95 * v_old + 0.05 * scaled * scaled

    def step(grad, state):
        m, v = moments(grad, state[0:rows], state[rows : 2 * rows])
        update = m / first_fix / (jnp.sqrt(v / second_fix) + 1e-08)
        return m, v, update, state[2 * rows :] * (1.0 - 0.0001 * 0.1) - 0.0001 * update

    for k in range(plan.zs):
        at = pl.ds(k * rows, rows)
        for flip, (sums, states) in enumerate(((sum_mine, state_mine), (sum_other, state_other))):
            out = step(sums[at, :], states[k])[3]
            start = pl.multiple_of((2 * k + (y ^ flip)) * rows, rows)
            weights_out[pl.ds(start, rows), :] = out.astype(BF16)

    m, v, update, master = step(sum_mine[pl.ds(pl.multiple_of(z * rows, rows), rows), :], state_mine[z])
    update_out[...] = update
    master_out[...] = master
    m_buf[...] = m
    v_buf[...] = v

    far[...] = jnp.zeros_like(far)

    def near(side, at_z, start):
        grad = sum_other[pl.ds(pl.multiple_of(at_z * rows + start, EDGE), EDGE), :]
        low = state_other[at_z, start : start + EDGE, :]
        high = state_other[at_z, rows + start : rows + start + EDGE, :]
        em, ev = moments(grad, low, high)
        far[side, 0], far[side, 1] = jnp.abs(em), jnp.abs(ev)

    def across(side, shard):
        for k in range(1, plan.groups, 2):
            @pl.when((shard >= 0) & (shard < plan.shards) & ((x ^ (k >> 1)) == shard // 2))
            def _():
                em, ev = moments(*(norms[k][8 + j * EDGE : 8 + (j + 1) * EDGE, :] for j in range(3)))
                far[side, 0], far[side, 1] = jnp.abs(em), jnp.abs(ev)

    shard = 2 * x + core

    @pl.when(y == 0)
    def _():
        near(1, z, 0)

        @pl.when(z > 0)
        def _():
            near(0, z - 1, rows - EDGE)

        @pl.when(z == 0)
        def _():
            across(0, shard - 1)

    @pl.when(y == 1)
    def _():
        near(0, z, rows - EDGE)

        @pl.when(z < plan.zs - 1)
        def _():
            near(1, z + 1, 0)

        @pl.when(z == plan.zs - 1)
        def _():
            across(1, shard + 1)

    for j in range(slots):
        low, high = max(0, (2 * j - 1) * EDGE), min(rows, (2 * j + 1) * EDGE)
        for which, (buf, table, norm_out) in enumerate(((m_buf, mt_out, mn_out), (v_buf, vt_out, vn_out))):
            values = buf[low:high, :]
            top = jnp.max(jnp.abs(values).reshape(-1, 8, LANES), axis=0)
            if j == 0:
                top = jnp.maximum(top, far[0, which])
            if j == slots - 1:
                top = jnp.maximum(top, far[1, which])
            top = jnp.max(top, keepdims=True)
            table[j] = top[0, 0]
            norm_out[low:high, :] = values / (top + 1e-06)


def on_device(grads, momentum_codes, variance_codes, momentum_scale, variance_scale, master, step):
    own_len = master.shape[0]
    slots = momentum_scale.shape[0]
    plan = Plan(own_len)
    rows, zs, groups = plan.rows, plan.zs, plan.groups
    struct = jax.ShapeDtypeStruct

    flat = grads.reshape(1, -1)
    arrived = plan.swap(half(plan, flat, 1), core=1)
    mine = half(plan, flat, 0)
    blocks = call(
        functools.partial(pair_kernel, plan), [struct((zs * rows, LANES), F32)] * groups, [mine, arrived]
    )
    arrived = [plan.swap(blocks[k], group=k) for k in range(1, groups)]
    part = call(sum_kernel, struct((zs * rows, LANES), F32), [blocks[0], *arrived])

    count = step[0].astype(F32)
    fixes = 1.0 - jnp.power(jnp.array([0.9, 0.95], F32), count)
    shape = (rows, LANES)
    state = call(
        functools.partial(state_kernel, plan),
        struct((3 * rows, LANES), F32),
        [momentum_codes.reshape(shape), variance_codes.reshape(shape), momentum_scale, variance_scale, master.reshape(shape)],
        in_specs=[VMEM, VMEM, SMEM, SMEM, VMEM],
    )
    states = [state] + [plan.swap(state, z=k) for k in range(1, zs)]
    state_mine = call(functools.partial(order_kernel, plan), struct((zs, 3 * rows, LANES), F32), states)
    state_other = plan.swap(state_mine, group=1)

    parts = [part] + [plan.swap(part, z=k) for k in range(1, zs)]
    send_rows = 8 + 3 * EDGE
    sum_mine, send = call(
        functools.partial(total_kernel, plan),
        [struct((zs * rows, LANES), F32), struct((send_rows, LANES), F32)],
        [*parts, state_mine],
    )
    sum_other = plan.swap(sum_mine, group=1)

    norm, relay = call(
        core_kernel, [struct((8, LANES), F32), struct((send_rows, LANES), F32)], [send, plan.swap(send, core=1)]
    )
    norms = [norm] + [plan.swap(relay if k % 2 else norm, group=k) for k in range(1, groups)]

    total_params = own_len * plan.devices
    own = struct((rows, LANES), F32)
    table = struct((slots,), F32)
    ins = [*norms, sum_mine, sum_other, state_mine, state_other, fixes]
    new_master, weights, update, mn, vn, mt, vt = call(
        functools.partial(main_kernel, plan, total_params),
        [own, struct((plan.reps * rows, LANES), BF16), own, own, own, table, table],
        ins,
        in_specs=[VMEM] * (len(ins) - 1) + [SMEM],
        out_specs=[VMEM] * 5 + [SMEM] * 2,
        scratch=[pltpu.VMEM(shape, F32), pltpu.VMEM(shape, F32), pltpu.VMEM((2, 2, EDGE, LANES), F32)],
    )
    return (
        new_master.reshape(-1),
        weights.reshape(-1),
        update.reshape(-1),
        mn.reshape(-1),
        vn.reshape(-1),
        mt,
        vt,
    )


def solution(mesh):
    own = P(ALL)
    in_specs = (P("shard", "rep", None), own, own, own, own, own, P())
    out_specs = (own, P("shard"), own, own, own, own, own)
    return jax.shard_map(on_device, mesh=mesh, in_specs=in_specs, out_specs=out_specs, check_vma=False)
```

```python
import functools

import jax
import jax.numpy as jnp
from jax import lax
from jax.experimental import pallas as pl
from jax.experimental.pallas import tpu as pltpu
from jax.sharding import PartitionSpec as P

BLOCK = 2048
LANES = 128
EDGE = BLOCK // 2 // LANES
ALL = ("shard", "rep")
BF16 = jnp.bfloat16
F32 = jnp.float32
VMEM = pl.BlockSpec(memory_space=pltpu.VMEM)
SMEM = pl.BlockSpec(memory_space=pltpu.SMEM)
ANY = pl.BlockSpec(memory_space=pl.ANY)
HBM = pl.BlockSpec(memory_space=pltpu.HBM)


class Plan:
    def __init__(self, own_len):
        self.shards = lax.axis_size("shard")
        self.reps = lax.axis_size("rep")
        self.devices = self.shards * self.reps
        self.xs = self.shards // 2
        self.zs = self.reps // 2
        self.groups = self.xs * 2
        self.rows = own_len // LANES

    def swap(self, value, core=0, z=0, group=0):
        x, y = group >> 1, group & 1
        mask = ((x << 1) | core) * self.reps + ((z << 1) | y)
        return lax.ppermute(value, ALL, [(i, i ^ mask) for i in range(self.devices)])


def place():
    shard, rep = lax.axis_index("shard"), lax.axis_index("rep")
    return shard // 2, shard % 2, rep // 2, rep % 2


def tree(values):
    values = list(values)
    while len(values) > 1:
        values = [a + b for a, b in zip(values[::2], values[1::2])]
    return values[0]


def call(kernel, outs, ins, in_specs=None, out_specs=None, scratch=(), limit=16):
    return pl.pallas_call(
        kernel,
        out_shape=outs,
        in_specs=in_specs or [VMEM] * len(ins),
        out_specs=out_specs or jax.tree.map(lambda _: VMEM, outs),
        scratch_shapes=list(scratch),
        compiler_params=pltpu.CompilerParams(vmem_limit_bytes=limit * 1024 * 1024),
    )(*ins)


def half_kernel(flip, count, length, x_ref, o_ref, buf, sem):
    _, core, _, _ = place()
    want = (core + flip) % 2
    rows = length // LANES
    copies = []
    for k in range(count):
        start = pl.multiple_of((2 * k + want) * length, length)
        copies.append(pltpu.make_async_copy(x_ref.at[:, pl.ds(start, length)], buf.at[k], sem.at[k]))
        copies[-1].start()
    for k in range(count):
        copies[k].wait()
        o_ref[pl.ds(k * rows, rows), :] = buf[k].astype(F32).reshape(rows, LANES).astype(BF16)


def half(plan, grads, flip):
    length = plan.reps * plan.rows * LANES
    return call(
        functools.partial(half_kernel, flip, plan.xs, length),
        jax.ShapeDtypeStruct((plan.xs * length // LANES, LANES), BF16),
        [grads],
        in_specs=[HBM],
        scratch=[pltpu.VMEM((plan.xs, 1, length), BF16), pltpu.SemaphoreType.DMA((plan.xs,))],
    )


def pair_kernel(plan, mine_ref, other_ref, *outs):
    x, _, _, y = place()
    for k, out in enumerate(outs):
        to_x, to_y = x ^ (k >> 1), y ^ (k & 1)
        for z in range(plan.zs):
            start = pl.multiple_of((to_x * plan.reps + 2 * z + to_y) * plan.rows, plan.rows)
            rows = pl.ds(start, plan.rows)
            out[pl.ds(z * plan.rows, plan.rows), :] = mine_ref[rows, :].astype(F32) + other_ref[rows, :].astype(F32)


def sum_kernel(*refs):
    refs[-1][...] = tree([r[...] for r in refs[:-1]])


def state_rows(plan, slots):
    return 2 * plan.rows + -(-2 * slots // 8) * 8


def state_kernel(plan, mc_ref, vc_ref, ms_ref, vs_ref, master_ref, _, o_ref):
    rows, slots = plan.rows, ms_ref.shape[0]
    o_ref[0:rows, :] = vc_ref[...].astype(F32) * 256.0 + (mc_ref[...].astype(F32) + 128.0)
    o_ref[rows : 2 * rows, :] = master_ref[...]
    for j in range(slots):
        o_ref[2 * rows + j : 2 * rows + j + 1, :] = jnp.full((1, LANES), ms_ref[j], F32)
        o_ref[2 * rows + slots + j : 2 * rows + slots + j + 1, :] = jnp.full((1, LANES), vs_ref[j], F32)


def old_moments(plan, state, slots, low, high):
    slot = (low + EDGE) // (2 * EDGE)
    m_at, v_at = 2 * plan.rows + slot, 2 * plan.rows + slots + slot
    pair = state[low:high, :]
    v_code = jnp.floor(pair * (1.0 / 256.0))
    m_code = pair - v_code * 256.0 - 128.0
    return m_code / 127.0 * state[m_at : m_at + 1, :], v_code / 255.0 * state[v_at : v_at + 1, :]


def pieces(plan, slots):
    return [(max(0, (2 * j - 1) * EDGE), min(plan.rows, (2 * j + 1) * EDGE)) for j in range(slots)]


def order_kernel(plan, *refs):
    _, _, z, _ = place()
    for k, ref in enumerate(refs[2:-1]):
        refs[-1][z ^ k] = ref[...]


def total_kernel(plan, slots, *refs):
    parts, (state_ref, sum_ref, send_ref) = refs[: plan.zs], refs[plan.zs :]
    _, _, _, y = place()
    total = tree([r[...] for r in parts])
    sum_ref[...] = total
    send_ref[0:8, :] = jnp.sum((total * total).reshape(-1, 8, LANES), axis=0)

    def edge(z, start):
        send_ref[8 : 8 + EDGE, :] = sum_ref[z * plan.rows + start : z * plan.rows + start + EDGE, :]
        old = old_moments(plan, state_ref.at[z], slots, start, start + EDGE)
        for k in range(2):
            send_ref[8 + (k + 1) * EDGE : 8 + (k + 2) * EDGE, :] = old[k]

    @pl.when(y == 0)
    def _():
        edge(0, 0)

    @pl.when(y == 1)
    def _():
        edge(plan.zs - 1, plan.rows - EDGE)


def core_kernel(mine_ref, other_ref, sum_ref, norm_ref, relay_ref, wide_ref):
    norm = mine_ref[0:8, :] + other_ref[0:8, :]
    norm_ref[...] = norm
    size = relay_ref.shape[0]
    for ref in (relay_ref, wide_ref):
        ref[0:8, :] = norm
        ref[8:size, :] = other_ref[8:, :]
    wide_ref[size:, :] = sum_ref[...]


def main_kernel(plan, total_params, *refs):
    norms, refs = refs[: plan.groups], refs[plan.groups :]
    (sum_mine, state_mine, state_other, fix_ref) = refs[:4]
    (master_out, weights_out, update_out, mn_out, vn_out, mt_out, vt_out) = refs[4:11]
    m_buf, v_buf, far = refs[11:]
    sum_other = norms[1].at[pl.ds(8 + 3 * EDGE, plan.zs * plan.rows)]
    x, core, z, y = place()
    rows = plan.rows
    slots = mt_out.shape[0]
    norm_sq = jnp.sum(tree([r[0:8, :] for r in norms]), keepdims=True)
    clip = jnp.minimum(1.0, float(total_params) ** 0.5 / (jnp.sqrt(norm_sq) + 1e-06))
    first_fix, second_fix = fix_ref[0], fix_ref[1]

    def moments(grad, m_old, v_old):
        scaled = grad * clip
        return 0.9 * m_old + 0.1 * scaled, 0.95 * v_old + 0.05 * scaled * scaled

    def step(grads, state, low, high):
        m, v = moments(grads[low:high, :], *old_moments(plan, state, slots, low, high))
        update = m / first_fix / (jnp.sqrt(v / second_fix) + 1e-08)
        master = state[rows + low : rows + high, :]
        return m, v, update, master * (1.0 - 0.0001 * 0.1) - 0.0001 * update

    for k in range(plan.zs):
        for flip, (sums, states) in enumerate(((sum_mine, state_mine), (sum_other, state_other))):
            start = pl.multiple_of((2 * k + (y ^ flip)) * rows, rows)
            grads = sums.at[pl.ds(k * rows, rows)]
            out = jnp.concatenate([step(grads, states.at[k], *piece)[3] for piece in pieces(plan, slots)], axis=0)
            weights_out[pl.ds(start, rows), :] = out.astype(BF16)

    grads = sum_mine.at[pl.ds(pl.multiple_of(z * rows, rows), rows)]
    for low, high in pieces(plan, slots):
        m, v, update, master = step(grads, state_mine.at[z], low, high)
        update_out[low:high, :] = update
        master_out[low:high, :] = master
        m_buf[low:high, :] = m
        v_buf[low:high, :] = v

    far[...] = jnp.zeros_like(far)

    def near(side, at_z, start):
        grad = sum_other[pl.ds(pl.multiple_of(at_z * rows + start, EDGE), EDGE), :]
        em, ev = moments(grad, *old_moments(plan, state_other.at[at_z], slots, start, start + EDGE))
        far[side, 0], far[side, 1] = jnp.abs(em), jnp.abs(ev)

    def across(side, shard):
        for k in range(1, plan.groups, 2):
            @pl.when((shard >= 0) & (shard < plan.shards) & ((x ^ (k >> 1)) == shard // 2))
            def _():
                em, ev = moments(*(norms[k][8 + j * EDGE : 8 + (j + 1) * EDGE, :] for j in range(3)))
                far[side, 0], far[side, 1] = jnp.abs(em), jnp.abs(ev)

    shard = 2 * x + core

    @pl.when(y == 0)
    def _():
        near(1, z, 0)

        @pl.when(z > 0)
        def _():
            near(0, z - 1, rows - EDGE)

        @pl.when(z == 0)
        def _():
            across(0, shard - 1)

    @pl.when(y == 1)
    def _():
        near(0, z, rows - EDGE)

        @pl.when(z < plan.zs - 1)
        def _():
            near(1, z + 1, 0)

        @pl.when(z == plan.zs - 1)
        def _():
            across(1, shard + 1)

    for j, (low, high) in enumerate(pieces(plan, slots)):
        for which, (buf, table, norm_out) in enumerate(((m_buf, mt_out, mn_out), (v_buf, vt_out, vn_out))):
            values = buf[low:high, :]
            top = jnp.max(jnp.abs(values).reshape(-1, 8, LANES), axis=0)
            if j == 0:
                top = jnp.maximum(top, far[0, which])
            if j == slots - 1:
                top = jnp.maximum(top, far[1, which])
            top = jnp.max(top, keepdims=True)
            table[j] = top[0, 0]
            norm_out[low:high, :] = values / (top + 1e-06)


def on_device(grads, momentum_codes, variance_codes, momentum_scale, variance_scale, master, step):
    own_len = master.shape[0]
    slots = momentum_scale.shape[0]
    plan = Plan(own_len)
    rows, zs, groups = plan.rows, plan.zs, plan.groups
    struct = jax.ShapeDtypeStruct

    flat = grads.reshape(1, -1)
    arrived = plan.swap(half(plan, flat, 1), core=1)
    mine = half(plan, flat, 0)
    blocks = call(
        functools.partial(pair_kernel, plan), [struct((zs * rows, LANES), F32)] * groups, [mine, arrived]
    )
    arrived = [plan.swap(blocks[k], group=k) for k in range(1, groups)]
    part = call(sum_kernel, struct((zs * rows, LANES), F32), [blocks[0], *arrived])

    count = step[0].astype(F32)
    fixes = 1.0 - jnp.power(jnp.array([0.9, 0.95], F32), count)
    shape = (rows, LANES)
    state = call(
        functools.partial(state_kernel, plan),
        struct((state_rows(plan, slots), LANES), F32),
        [momentum_codes.reshape(shape), variance_codes.reshape(shape), momentum_scale, variance_scale, master.reshape(shape), blocks[0]],
        in_specs=[VMEM, VMEM, SMEM, SMEM, VMEM, ANY],
    )
    states = [state] + [plan.swap(state, z=k) for k in range(1, zs)]

    parts = [part] + [plan.swap(part, z=k) for k in range(1, zs)]
    state_mine = call(
        functools.partial(order_kernel, plan),
        struct((zs, state_rows(plan, slots), LANES), F32),
        [parts[1], fixes, *states],
        [ANY, SMEM] + [VMEM] * zs,
    )
    state_other = plan.swap(state_mine, group=1)
    send_rows = 8 + 3 * EDGE
    sum_mine, send = call(
        functools.partial(total_kernel, plan, slots),
        [struct((zs * rows, LANES), F32), struct((send_rows, LANES), F32)],
        [*parts, state_mine],
    )
    norm, relay, wide = call(
        core_kernel,
        [struct((8, LANES), F32), struct((send_rows, LANES), F32), struct((send_rows + zs * rows, LANES), F32)],
        [send, plan.swap(send, core=1), sum_mine],
    )
    wide = plan.swap(wide, group=1)
    norms = [norm, wide] + [plan.swap(relay if k % 2 else norm, group=k) for k in range(2, groups)]

    total_params = own_len * plan.devices
    own = struct((rows, LANES), F32)
    table = struct((slots,), F32)
    ins = [*norms, sum_mine, state_mine, state_other, fixes]
    new_master, weights, update, mn, vn, mt, vt = call(
        functools.partial(main_kernel, plan, total_params),
        [own, struct((plan.reps * rows, LANES), BF16), own, own, own, table, table],
        ins,
        in_specs=[VMEM] * (len(ins) - 1) + [SMEM],
        out_specs=[VMEM] * 5 + [SMEM] * 2,
        scratch=[pltpu.VMEM(shape, F32), pltpu.VMEM(shape, F32), pltpu.VMEM((2, 2, EDGE, LANES), F32)],
    )
    return (
        new_master.reshape(-1),
        weights.reshape(-1),
        update.reshape(-1),
        mn.reshape(-1),
        vn.reshape(-1),
        mt,
        vt,
    )


def solution(mesh):
    own = P(ALL)
    in_specs = (P("shard", "rep", None), own, own, own, own, own, P())
    out_specs = (own, P("shard"), own, own, own, own, own)
    return jax.shard_map(on_device, mesh=mesh, in_specs=in_specs, out_specs=out_specs, check_vma=False)
```

```python
import functools

import jax
import jax.numpy as jnp
from jax import lax
from jax.experimental import pallas as pl
from jax.experimental.pallas import tpu as pltpu
from jax.sharding import PartitionSpec as P

BLOCK = 2048
LANES = 128
EDGE = BLOCK // 2 // LANES
ALL = ("shard", "rep")
BF16 = jnp.bfloat16
F32 = jnp.float32
VMEM = pl.BlockSpec(memory_space=pltpu.VMEM)
SMEM = pl.BlockSpec(memory_space=pltpu.SMEM)
ANY = pl.BlockSpec(memory_space=pl.ANY)
HBM = pl.BlockSpec(memory_space=pltpu.HBM)


class Plan:
    def __init__(self, own_len):
        self.shards = lax.axis_size("shard")
        self.reps = lax.axis_size("rep")
        self.devices = self.shards * self.reps
        self.xs = self.shards // 2
        self.zs = self.reps // 2
        self.groups = self.xs * 2
        self.rows = own_len // LANES

    def swap(self, value, core=0, z=0, group=0):
        x, y = group >> 1, group & 1
        mask = ((x << 1) | core) * self.reps + ((z << 1) | y)
        return lax.ppermute(value, ALL, [(i, i ^ mask) for i in range(self.devices)])


def place():
    shard, rep = lax.axis_index("shard"), lax.axis_index("rep")
    return shard // 2, shard % 2, rep // 2, rep % 2


def tree(values):
    values = list(values)
    while len(values) > 1:
        values = [a + b for a, b in zip(values[::2], values[1::2])]
    return values[0]


def call(kernel, outs, ins, in_specs=None, out_specs=None, scratch=(), limit=16):
    limit = int(limit * 1024 * 1024)
    return pl.pallas_call(
        kernel,
        out_shape=outs,
        in_specs=in_specs or [VMEM] * len(ins),
        out_specs=out_specs or jax.tree.map(lambda _: VMEM, outs),
        scratch_shapes=list(scratch),
        compiler_params=pltpu.CompilerParams(vmem_limit_bytes=limit),
    )(*ins)


def half_kernel(flip, count, length, x_ref, o_ref, buf, sem):
    _, core, _, _ = place()
    want = (core + flip) % 2
    rows = length // LANES
    copies = []
    for k in range(count):
        start = pl.multiple_of((2 * k + want) * length, length)
        copies.append(pltpu.make_async_copy(x_ref.at[:, pl.ds(start, length)], buf.at[k], sem.at[k]))
        copies[-1].start()
    for k in range(count):
        copies[k].wait()
        o_ref[pl.ds(k * rows, rows), :] = buf[k].astype(F32).reshape(rows, LANES).astype(BF16)


def half_call(plan, kernel, outs, ins):
    length = plan.reps * plan.rows * LANES
    return call(
        kernel,
        [jax.ShapeDtypeStruct((plan.xs * length // LANES, LANES), BF16), *outs],
        ins,
        in_specs=[ANY] * len(ins),
        scratch=[
            pltpu.VMEM((plan.xs, 1, length), BF16),
            pltpu.SemaphoreType.DMA((plan.xs,)),
            *(pltpu.VMEM(x.shape, x.dtype) for x in ins[1:]),
            *([pltpu.SemaphoreType.DMA((len(ins) - 1,))] if ins[1:] else []),
        ],
        limit=53.25,
    )


def own_kernel(plan, x_ref, o_ref, buf, sem):
    half_kernel(0, plan.xs, plan.reps * plan.rows * LANES, x_ref, o_ref, buf, sem)


def other_kernel(plan, x_ref, o_ref, buf, sem):
    half_kernel(1, plan.xs, plan.reps * plan.rows * LANES, x_ref, o_ref, buf, sem)


def pair_kernel(plan, mine_ref, other_ref, *outs):
    x, _, _, y = place()
    for k, out in enumerate(outs):
        to_x, to_y = x ^ (k >> 1), y ^ (k & 1)
        for z in range(plan.zs):
            start = pl.multiple_of((to_x * plan.reps + 2 * z + to_y) * plan.rows, plan.rows)
            rows = pl.ds(start, plan.rows)
            out[pl.ds(z * plan.rows, plan.rows), :] = mine_ref[rows, :].astype(F32) + other_ref[rows, :].astype(F32)


def part_kernel(*refs):
    *terms, low_ref, high_ref = refs
    half = low_ref.shape[0]
    low_ref[...] = tree([r[:half, :] for r in terms])
    high_ref[...] = tree([r[half:, :] for r in terms])


def two_kernel(low_ref, low_other, high_ref, high_other, low_out, high_out):
    low_out[...] = low_ref[...] + low_other[...]
    high_out[...] = high_ref[...] + high_other[...]


def state_rows(plan, slots):
    return 2 * plan.rows + scale_rows(slots)


def scale_rows(slots):
    return -(-(slots + 2) // 8) * 8


def power(base, count):
    value, square = jnp.ones(count.shape, F32), jnp.full(count.shape, base, F32)
    for bit in range(8):
        value = jnp.where((count >> bit) & 1 == 1, value * square, value)
        square = square * square
    return value


def state_kernel(plan, mc_ref, vc_ref, ms_ref, vs_ref, master_ref, _, o_ref):
    o_ref = o_ref.at[0]
    rows, slots = plan.rows, ms_ref.shape[1]
    o_ref[0:rows, :] = vc_ref[...].astype(F32) * 256.0 + (mc_ref[...].astype(F32) + 128.0)
    o_ref[rows : 2 * rows, :] = master_ref[...]
    lane = lax.broadcasted_iota(jnp.int32, (1, LANES), 1)
    for j in range(slots):
        scales = jnp.where(lane < LANES // 2, ms_ref[:, j : j + 1], vs_ref[:, j : j + 1])
        o_ref[2 * rows + j : 2 * rows + j + 1, :] = scales


def old_moments(state, scales, low, high):
    slot = (low + EDGE) // (2 * EDGE)
    scale = scales[slot : slot + 1, :]
    pair = state[low:high, :]
    v_code = jnp.floor(pair * (1.0 / 256.0))
    m_code = pair - v_code * 256.0 - 128.0
    return m_code / 127.0 * scale[:, 0:1], v_code / 255.0 * scale[:, LANES // 2 : LANES // 2 + 1]


def pieces(plan, slots):
    return [(max(0, (2 * j - 1) * EDGE), min(plan.rows, (2 * j + 1) * EDGE)) for j in range(slots)]


def order_kernel(plan, slots, step_ref, _, *refs):
    *states, o_ref, send_ref = refs
    _, _, z, _ = place()
    for k, ref in enumerate(states):
        o_ref[z ^ k] = ref[0]
        send_ref[z ^ k] = ref[0, : send_ref.shape[1], :]
    count = jnp.broadcast_to(step_ref[...], (1, LANES))
    for j, base in enumerate((0.9, 0.95)):
        at = 2 * plan.rows + slots + j
        for i in range(plan.zs):
            o_ref[i, at : at + 1, :] = 1.0 - power(base, count)


def squares(values):
    return jnp.sum((values * values).reshape(-1, 8, LANES), axis=0)


def total_kernel(plan, *refs):
    low_ref, low_other, high_ref, high_other, state_ref, sum_ref, send_ref = refs
    _, _, _, y = place()
    half = low_ref.shape[0]
    low, high = low_ref[...] + low_other[...], high_ref[...] + high_other[...]
    sum_ref[:half, :] = low
    sum_ref[half:, :] = high
    send_ref[0:8, :] = squares(low) + squares(high)

    def edge(z, start):
        send_ref[8 : 8 + EDGE, :] = sum_ref[z * plan.rows + start : z * plan.rows + start + EDGE, :]
        state = state_ref.at[z]
        old = old_moments(state, state.at[2 * plan.rows :], start, start + EDGE)
        for k in range(2):
            send_ref[8 + (k + 1) * EDGE : 8 + (k + 2) * EDGE, :] = old[k]

    @pl.when(y == 0)
    def _():
        edge(0, 0)

    @pl.when(y == 1)
    def _():
        edge(plan.zs - 1, plan.rows - EDGE)


def core_kernel(plan, mine_ref, other_ref, sum_ref, state_ref, norm_ref, relay_ref, wide_ref):
    norm = mine_ref[0:8, :] + other_ref[0:8, :]
    norm_ref[...] = norm
    size = relay_ref.shape[0]
    for ref in (relay_ref, wide_ref):
        ref[0:8, :] = norm
        ref[8:size, :] = other_ref[8:, :]
    end = size + sum_ref.shape[0]
    wide_ref[size:end, :] = sum_ref[...]
    scales = state_ref.shape[1] - 2 * plan.rows
    for z in range(plan.zs):
        wide_ref[end + z * scales : end + (z + 1) * scales, :] = state_ref[z, 2 * plan.rows :, :]


def main_kernel(plan, total_params, *refs):
    norms, refs = refs[: plan.groups], refs[plan.groups :]
    (sum_mine, state_mine, state_other) = refs[:3]
    (master_out, weights_out, update_out, mn_out, vn_out, mt_out, vt_out) = refs[3:10]
    m_buf, v_buf, far = refs[10:]
    sums_at, scales_at = 8 + 3 * EDGE, 8 + 3 * EDGE + plan.zs * plan.rows
    sum_other = norms[1].at[sums_at:scales_at]
    x, core, z, y = place()
    rows = plan.rows
    slots = mt_out.shape[0]
    norm_sq = jnp.sum(tree([r[0:8, :] for r in norms]), keepdims=True)
    clip = jnp.minimum(1.0, float(total_params) ** 0.5 / (jnp.sqrt(norm_sq) + 1e-06))
    def scales_mine(k):
        return state_mine.at[k, 2 * rows :]

    def scales_other(k):
        size = scale_rows(slots)
        return norms[1].at[pl.ds(scales_at + k * size, size)]

    at = 2 * rows + slots
    first_fix, second_fix = state_mine[0, at : at + 1, :], state_mine[0, at + 1 : at + 2, :]

    def moments(grad, m_old, v_old):
        scaled = grad * clip
        return 0.9 * m_old + 0.1 * scaled, 0.95 * v_old + 0.05 * scaled * scaled

    def step(grads, state, scales, low, high):
        m, v = moments(grads[low:high, :], *old_moments(state, scales, low, high))
        update = m / first_fix / (jnp.sqrt(v / second_fix) + 1e-08)
        master = state[rows + low : rows + high, :]
        return m, v, update, master * (1.0 - 0.0001 * 0.1) - 0.0001 * update

    for k in range(plan.zs):
        sides = ((sum_mine, state_mine, scales_mine), (sum_other, state_other, scales_other))
        for flip, (sums, states, scales) in enumerate(sides):
            start = pl.multiple_of((2 * k + (y ^ flip)) * rows, rows)
            grads = sums.at[pl.ds(k * rows, rows)]
            out = jnp.concatenate([step(grads, states.at[k], scales(k), *piece)[3] for piece in pieces(plan, slots)], axis=0)
            weights_out[pl.ds(start, rows), :] = out.astype(BF16)

    grads = sum_mine.at[pl.ds(pl.multiple_of(z * rows, rows), rows)]
    for low, high in pieces(plan, slots):
        m, v, update, master = step(grads, state_mine.at[z], scales_mine(z), low, high)
        update_out[low:high, :] = update
        master_out[low:high, :] = master
        m_buf[low:high, :] = m
        v_buf[low:high, :] = v

    far[...] = jnp.zeros_like(far)

    def near(side, at_z, start):
        grad = sum_other[pl.ds(pl.multiple_of(at_z * rows + start, EDGE), EDGE), :]
        em, ev = moments(grad, *old_moments(state_other.at[at_z], scales_other(at_z), start, start + EDGE))
        far[side, 0], far[side, 1] = jnp.abs(em), jnp.abs(ev)

    def across(side, shard):
        for k in range(1, plan.groups, 2):
            @pl.when((shard >= 0) & (shard < plan.shards) & ((x ^ (k >> 1)) == shard // 2))
            def _():
                em, ev = moments(*(norms[k][8 + j * EDGE : 8 + (j + 1) * EDGE, :] for j in range(3)))
                far[side, 0], far[side, 1] = jnp.abs(em), jnp.abs(ev)

    shard = 2 * x + core

    @pl.when(y == 0)
    def _():
        near(1, z, 0)

        @pl.when(z > 0)
        def _():
            near(0, z - 1, rows - EDGE)

        @pl.when(z == 0)
        def _():
            across(0, shard - 1)

    @pl.when(y == 1)
    def _():
        near(0, z, rows - EDGE)

        @pl.when(z < plan.zs - 1)
        def _():
            near(1, z + 1, 0)

        @pl.when(z == plan.zs - 1)
        def _():
            across(1, shard + 1)

    for j, (low, high) in enumerate(pieces(plan, slots)):
        for which, (buf, table, norm_out) in enumerate(((m_buf, mt_out, mn_out), (v_buf, vt_out, vn_out))):
            values = buf[low:high, :]
            top = jnp.max(jnp.abs(values).reshape(-1, 8, LANES), axis=0)
            if j == 0:
                top = jnp.maximum(top, far[0, which])
            if j == slots - 1:
                top = jnp.maximum(top, far[1, which])
            top = jnp.max(top, keepdims=True)
            table[j] = top[0, 0]
            norm_out[low:high, :] = values / (top + 1e-06)


def on_device(grads, momentum_codes, variance_codes, momentum_scale, variance_scale, master, step):
    own_len = master.shape[0]
    slots = momentum_scale.shape[0]
    plan = Plan(own_len)
    rows, zs, groups = plan.rows, plan.zs, plan.groups
    struct = jax.ShapeDtypeStruct

    shape = (rows, LANES)
    state_shape = (state_rows(plan, slots), LANES)
    part_shape = struct((zs * rows, LANES), F32)
    half_shape = struct((zs * rows // 2, LANES), F32)

    flat = grads.reshape(1, -1)
    (send,) = half_call(plan, functools.partial(other_kernel, plan), [], [flat])
    arrived = plan.swap(send, core=1)
    (mine,) = half_call(plan, functools.partial(own_kernel, plan), [], [flat])
    blocks = call(functools.partial(pair_kernel, plan), [part_shape] * groups, [mine, arrived])

    sums = [plan.swap(blocks[k], group=k) for k in range(1, groups)]

    low, high = call(part_kernel, [half_shape] * 2, [blocks[0], *sums])

    states = call(
        functools.partial(state_kernel, plan),
        struct((1, *state_shape), F32),
        [
            momentum_codes.reshape(shape),
            variance_codes.reshape(shape),
            momentum_scale.reshape(1, slots),
            variance_scale.reshape(1, slots),
            master.reshape(shape),
            blocks[0],
        ],
        [VMEM] * 5 + [ANY],
    )
    near = [states] + [plan.swap(states, z=k) for k in range(1, zs)]

    gate = low
    bits = (zs - 1).bit_length()
    for bit in range(bits):
        high_other = plan.swap(high, z=1 << (bits - 1 - bit))
        low_other = plan.swap(low, z=1 << bit)
        if bit < bits - 1:
            low, high = call(two_kernel, [half_shape] * 2, [low, low_other, high, high_other])
    state_mine, state_send = call(
        functools.partial(order_kernel, plan, slots),
        [struct((zs, *state_shape), F32), struct((zs, 2 * rows, LANES), F32)],
        [step.reshape(1, 1), gate, *near],
        [VMEM, ANY] + [VMEM] * zs,
    )
    state_other = plan.swap(state_send, group=1)
    send_rows = 8 + 3 * EDGE
    sum_mine, send = call(
        functools.partial(total_kernel, plan),
        [part_shape, struct((send_rows, LANES), F32)],
        [low, low_other, high, high_other, state_mine],
    )

    wide_rows = send_rows + zs * (rows + scale_rows(slots))
    norm, relay, wide = call(
        functools.partial(core_kernel, plan),
        [struct((n, LANES), F32) for n in (8, send_rows, wide_rows)],
        [send, plan.swap(send, core=1), sum_mine, state_mine],
    )
    wide = plan.swap(wide, group=1)
    norms = [norm, wide] + [plan.swap(relay if k % 2 else norm, group=k) for k in range(2, groups)]

    total_params = own_len * plan.devices
    own = struct((rows, LANES), F32)
    table = struct((slots,), F32)
    ins = [*norms, sum_mine, state_mine, state_other]
    new_master, weights, update, mn, vn, mt, vt = call(
        functools.partial(main_kernel, plan, total_params),
        [own, struct((plan.reps * rows, LANES), BF16), own, own, own, table, table],
        ins,
        out_specs=[VMEM] * 5 + [SMEM] * 2,
        scratch=[pltpu.VMEM(shape, F32), pltpu.VMEM(shape, F32), pltpu.VMEM((2, 2, EDGE, LANES), F32)],
    )
    return (
        new_master.reshape(-1),
        weights.reshape(-1),
        update.reshape(-1),
        mn.reshape(-1),
        vn.reshape(-1),
        mt,
        vt,
    )


def solution(mesh):
    own = P(ALL)
    in_specs = (P("shard", "rep", None), own, own, own, own, own, P())
    out_specs = (own, P("shard"), own, own, own, own, own)
    return jax.shard_map(on_device, mesh=mesh, in_specs=in_specs, out_specs=out_specs, check_vma=False)
```

```python
import functools

import jax
import jax.numpy as jnp
from jax import lax
from jax.experimental import pallas as pl
from jax.experimental.pallas import tpu as pltpu
from jax.sharding import PartitionSpec as P

BLOCK = 2048
LANES = 128
EDGE = BLOCK // 2 // LANES
ALL = ("shard", "rep")
BF16 = jnp.bfloat16
F32 = jnp.float32
VMEM = pl.BlockSpec(memory_space=pltpu.VMEM)
SMEM = pl.BlockSpec(memory_space=pltpu.SMEM)
ANY = pl.BlockSpec(memory_space=pl.ANY)
HBM = pl.BlockSpec(memory_space=pltpu.HBM)


class Plan:
    def __init__(self, own_len):
        self.shards = lax.axis_size("shard")
        self.reps = lax.axis_size("rep")
        self.devices = self.shards * self.reps
        self.xs = self.shards // 2
        self.zs = self.reps // 2
        self.groups = self.xs * 2
        self.rows = own_len // LANES

    def swap(self, value, core=0, z=0, group=0):
        x, y = group >> 1, group & 1
        mask = ((x << 1) | core) * self.reps + ((z << 1) | y)
        return lax.ppermute(value, ALL, [(i, i ^ mask) for i in range(self.devices)])


def place():
    shard, rep = lax.axis_index("shard"), lax.axis_index("rep")
    return shard // 2, shard % 2, rep // 2, rep % 2


def tree(values):
    values = list(values)
    while len(values) > 1:
        values = [a + b for a, b in zip(values[::2], values[1::2])]
    return values[0]


def call(kernel, outs, ins, in_specs=None, out_specs=None, scratch=(), limit=16):
    limit = int(limit * 1024 * 1024)
    return pl.pallas_call(
        kernel,
        out_shape=outs,
        in_specs=in_specs or [VMEM] * len(ins),
        out_specs=out_specs or jax.tree.map(lambda _: VMEM, outs),
        scratch_shapes=list(scratch),
        compiler_params=pltpu.CompilerParams(vmem_limit_bytes=limit),
    )(*ins)


def half_kernel(flip, count, length, x_ref, o_ref, buf, sem):
    _, core, _, _ = place()
    want = (core + flip) % 2
    rows = length // LANES
    copies = []
    for k in range(count):
        start = pl.multiple_of((2 * k + want) * length, length)
        copies.append(pltpu.make_async_copy(x_ref.at[:, pl.ds(start, length)], buf.at[k], sem.at[k]))
        copies[-1].start()
    for k in range(count):
        copies[k].wait()
        o_ref[pl.ds(k * rows, rows), :] = buf[k].astype(F32).reshape(rows, LANES).astype(BF16)


def half_call(plan, kernel, outs, ins):
    length = plan.reps * plan.rows * LANES
    return call(
        kernel,
        [jax.ShapeDtypeStruct((plan.xs * length // LANES, LANES), BF16), *outs],
        ins,
        in_specs=[ANY] * len(ins),
        scratch=[
            pltpu.VMEM((plan.xs, 1, length), BF16),
            pltpu.SemaphoreType.DMA((plan.xs,)),
            *(pltpu.VMEM(x.shape, x.dtype) for x in ins[1:]),
            *([pltpu.SemaphoreType.DMA((len(ins) - 1,))] if ins[1:] else []),
        ],
        limit=53.25,
    )


def own_kernel(plan, x_ref, o_ref, buf, sem):
    half_kernel(0, plan.xs, plan.reps * plan.rows * LANES, x_ref, o_ref, buf, sem)


def other_kernel(plan, x_ref, o_ref, buf, sem):
    half_kernel(1, plan.xs, plan.reps * plan.rows * LANES, x_ref, o_ref, buf, sem)


def pair_kernel(plan, mine_ref, other_ref, *outs):
    x, _, _, y = place()
    for k, out in enumerate(outs):
        to_x, to_y = x ^ (k >> 1), y ^ (k & 1)
        for z in range(plan.zs):
            start = pl.multiple_of((to_x * plan.reps + 2 * z + to_y) * plan.rows, plan.rows)
            rows = pl.ds(start, plan.rows)
            out[pl.ds(z * plan.rows, plan.rows), :] = mine_ref[rows, :].astype(F32) + other_ref[rows, :].astype(F32)


def part_kernel(*refs):
    *terms, low_ref, high_ref = refs
    half = low_ref.shape[0]
    low_ref[...] = tree([r[:half, :] for r in terms])
    high_ref[...] = tree([r[half:, :] for r in terms])


def add_kernel(mine_ref, other_ref, _, o_ref):
    o_ref[...] = mine_ref[...] + other_ref[...]


def state_rows(plan, slots):
    return 2 * plan.rows + scale_rows(slots)


def scale_rows(slots):
    return -(-slots // 8) * 8


def power(base, count):
    value, square = jnp.ones(count.shape, F32), jnp.full(count.shape, base, F32)
    for bit in range(8):
        value = jnp.where((count >> bit) & 1 == 1, value * square, value)
        square = square * square
    return value


def state_kernel(plan, mc_ref, vc_ref, ms_ref, vs_ref, master_ref, _, o_ref):
    o_ref = o_ref.at[0]
    rows, slots = plan.rows, ms_ref.shape[1]
    o_ref[0:rows, :] = vc_ref[...].astype(F32) * 256.0 + (mc_ref[...].astype(F32) + 128.0)
    o_ref[rows : 2 * rows, :] = master_ref[...]
    lane = lax.broadcasted_iota(jnp.int32, (1, LANES), 1)
    for j in range(slots):
        scales = jnp.where(lane < LANES // 2, ms_ref[:, j : j + 1], vs_ref[:, j : j + 1])
        o_ref[2 * rows + j : 2 * rows + j + 1, :] = scales


def decayed(state, scales, low, high):
    slot = (low + EDGE) // (2 * EDGE)
    scale = scales[slot : slot + 1, :]
    pair = state[low:high, :]
    v_code = jnp.floor(pair * (1.0 / 256.0))
    m_code = pair - (v_code * 256.0 + 128.0)
    m_scale, v_scale = scale[:, 0:1] * (0.9 / 127.0), scale[:, LANES // 2 : LANES // 2 + 1] * (0.95 / 255.0)
    return m_code * m_scale, v_code * v_scale


def pieces(plan, slots):
    return [(max(0, (2 * j - 1) * EDGE), min(plan.rows, (2 * j + 1) * EDGE)) for j in range(slots)]


def order_kernel(plan, _, *refs):
    *states, o_ref, send_ref = refs
    _, _, z, _ = place()
    for k, ref in enumerate(states):
        o_ref[z ^ k] = ref[0]
        send_ref[z ^ k] = ref[0, : send_ref.shape[1], :]


def token_kernel(x_ref, *refs):
    refs[-1][...] = x_ref[0:8, :]


def fix_kernel(step_ref, _, o_ref):
    count = jnp.broadcast_to(step_ref[...], (1, LANES))
    for j, base in enumerate((0.9, 0.95)):
        o_ref[j : j + 1, :] = 1.0 / (1.0 - power(base, count))


def squares(values):
    return jnp.sum((values * values).reshape(-1, 8, LANES), axis=0)


def total_kernel(plan, *refs):
    low_ref, low_other, high_ref, high_other, state_ref, sum_ref, send_ref = refs
    _, _, _, y = place()
    half = low_ref.shape[0]
    low, high = low_ref[...] + low_other[...], high_ref[...] + high_other[...]
    sum_ref[:half, :] = low
    sum_ref[half:, :] = high
    send_ref[0:8, :] = squares(low) + squares(high)

    def edge(z, start):
        send_ref[8 : 8 + EDGE, :] = sum_ref[z * plan.rows + start : z * plan.rows + start + EDGE, :]
        state = state_ref.at[z]
        old = decayed(state, state.at[2 * plan.rows :], start, start + EDGE)
        for k in range(2):
            send_ref[8 + (k + 1) * EDGE : 8 + (k + 2) * EDGE, :] = old[k]

    @pl.when(y == 0)
    def _():
        edge(0, 0)

    @pl.when(y == 1)
    def _():
        edge(plan.zs - 1, plan.rows - EDGE)


def core_kernel(plan, mine_ref, other_ref, sum_ref, state_ref, norm_ref, relay_ref, wide_ref):
    norm = mine_ref[0:8, :] + other_ref[0:8, :]
    norm_ref[...] = norm
    size = relay_ref.shape[0]
    for ref in (relay_ref, wide_ref):
        ref[0:8, :] = norm
        ref[8:size, :] = other_ref[8:, :]
    end = size + sum_ref.shape[0]
    wide_ref[size:end, :] = sum_ref[...]
    scales = state_ref.shape[1] - 2 * plan.rows
    for z in range(plan.zs):
        wide_ref[end + z * scales : end + (z + 1) * scales, :] = state_ref[z, 2 * plan.rows :, :]


def main_kernel(plan, total_params, *refs):
    norms, refs = refs[: plan.groups], refs[plan.groups :]
    (sum_mine, state_mine, state_other, fix_ref) = refs[:4]
    (master_out, weights_out, update_out, mn_out, vn_out, mt_out, vt_out) = refs[4:11]
    m_buf, v_buf, far = refs[11:]
    sums_at, scales_at = 8 + 3 * EDGE, 8 + 3 * EDGE + plan.zs * plan.rows
    sum_other = norms[1].at[sums_at:scales_at]
    x, core, z, y = place()
    rows = plan.rows
    slots = mt_out.shape[1]
    norm_sq = jnp.sum(tree([r[0:8, :] for r in norms]), keepdims=True)
    clip = jnp.minimum(1.0, float(total_params) ** 0.5 / (jnp.sqrt(norm_sq) + 1e-06))
    def scales_mine(k):
        return state_mine.at[k, 2 * rows :]

    def scales_other(k):
        size = scale_rows(slots)
        return norms[1].at[pl.ds(scales_at + k * size, size)]

    first, second = fix_ref[0:1, :], fix_ref[1:2, :]

    def moments(grad, m_decayed, v_decayed):
        scaled = grad * clip
        return m_decayed + 0.1 * scaled, v_decayed + 0.05 * scaled * scaled

    def step(grads, state, scales, low, high):
        m, v = moments(grads[low:high, :], *decayed(state, scales, low, high))
        update = m * first / (jnp.sqrt(v * second) + 1e-08)
        master = state[rows + low : rows + high, :]
        return m, v, update, master * (1.0 - 0.0001 * 0.1) - 0.0001 * update

    for k in range(plan.zs):
        sides = ((sum_mine, state_mine, scales_mine), (sum_other, state_other, scales_other))
        for flip, (sums, states, scales) in enumerate(sides):
            start = pl.multiple_of((2 * k + (y ^ flip)) * rows, rows)
            grads = sums.at[pl.ds(k * rows, rows)]
            out = jnp.concatenate([step(grads, states.at[k], scales(k), *piece)[3] for piece in pieces(plan, slots)], axis=0)
            weights_out[pl.ds(start, rows), :] = out.astype(BF16)

    grads = sum_mine.at[pl.ds(pl.multiple_of(z * rows, rows), rows)]
    for low, high in pieces(plan, slots):
        m, v, update, master = step(grads, state_mine.at[z], scales_mine(z), low, high)
        update_out[low:high, :] = update
        master_out[low:high, :] = master
        m_buf[low:high, :] = m
        v_buf[low:high, :] = v

    far[...] = jnp.zeros_like(far)

    def near(side, at_z, start):
        grad = sum_other[pl.ds(pl.multiple_of(at_z * rows + start, EDGE), EDGE), :]
        em, ev = moments(grad, *decayed(state_other.at[at_z], scales_other(at_z), start, start + EDGE))
        far[side, 0], far[side, 1] = jnp.abs(em), jnp.abs(ev)

    def across(side, shard):
        for k in range(1, plan.groups, 2):
            @pl.when((shard >= 0) & (shard < plan.shards) & ((x ^ (k >> 1)) == shard // 2))
            def _():
                em, ev = moments(*(norms[k][8 + j * EDGE : 8 + (j + 1) * EDGE, :] for j in range(3)))
                far[side, 0], far[side, 1] = jnp.abs(em), jnp.abs(ev)

    shard = 2 * x + core

    @pl.when(y == 0)
    def _():
        near(1, z, 0)

        @pl.when(z > 0)
        def _():
            near(0, z - 1, rows - EDGE)

        @pl.when(z == 0)
        def _():
            across(0, shard - 1)

    @pl.when(y == 1)
    def _():
        near(0, z, rows - EDGE)

        @pl.when(z < plan.zs - 1)
        def _():
            near(1, z + 1, 0)

        @pl.when(z == plan.zs - 1)
        def _():
            across(1, shard + 1)

    lane = lax.broadcasted_iota(jnp.int32, (1, LANES), 1)
    for which, (buf, table, norm_out) in enumerate(((m_buf, mt_out, mn_out), (v_buf, vt_out, vn_out))):
        line = jnp.zeros((1, LANES), F32)
        for j, (low, high) in enumerate(pieces(plan, slots)):
            values = buf[low:high, :]
            top = jnp.max(jnp.abs(values).reshape(-1, 8, LANES), axis=0)
            if j == 0:
                top = jnp.maximum(top, far[0, which])
            if j == slots - 1:
                top = jnp.maximum(top, far[1, which])
            top = jnp.max(top, keepdims=True)
            line = jnp.where(lane == j, top, line)
            norm_out[low:high, :] = values / (top + 1e-06)
        table[...] = line[:, :slots]


def on_device(grads, momentum_codes, variance_codes, momentum_scale, variance_scale, master, step):
    own_len = master.shape[0]
    slots = momentum_scale.shape[0]
    plan = Plan(own_len)
    rows, zs, groups = plan.rows, plan.zs, plan.groups
    struct = jax.ShapeDtypeStruct

    shape = (rows, LANES)
    state_shape = (state_rows(plan, slots), LANES)
    part_shape = struct((zs * rows, LANES), F32)
    half_shape = struct((zs * rows // 2, LANES), F32)

    flat = grads.reshape(1, -1)
    (send,) = half_call(plan, functools.partial(other_kernel, plan), [], [flat])
    arrived = plan.swap(send, core=1)
    (mine,) = half_call(plan, functools.partial(own_kernel, plan), [], [flat])
    blocks = call(functools.partial(pair_kernel, plan), [part_shape] * groups, [mine, arrived])

    sums = [plan.swap(blocks[k], group=k) for k in range(1, groups)]

    low, high = call(part_kernel, [half_shape] * 2, [blocks[0], *sums])

    states = call(
        functools.partial(state_kernel, plan),
        struct((1, *state_shape), F32),
        [
            momentum_codes.reshape(shape),
            variance_codes.reshape(shape),
            momentum_scale.reshape(1, slots),
            variance_scale.reshape(1, slots),
            master.reshape(shape),
            blocks[0],
        ],
        [VMEM] * 5 + [ANY],
    )
    near = [states] + [plan.swap(states, z=k) for k in range(1, zs)]

    gate = low
    bits = (zs - 1).bit_length()
    for bit in range(bits):
        high_other = plan.swap(high, z=1 << (bits - 1 - bit))
        low_other = plan.swap(low, z=1 << bit)
        if bit < bits - 1:
            high = call(add_kernel, half_shape, [high, high_other, low], [VMEM, VMEM, ANY])
            low = call(add_kernel, half_shape, [low, low_other, high], [VMEM, VMEM, ANY])
    gate = call(token_kernel, struct((8, LANES), F32), [gate, *near[2:]], [VMEM] + [ANY] * (zs - 2))
    state_mine, state_send = call(
        functools.partial(order_kernel, plan),
        [struct((zs, *state_shape), F32), struct((zs, 2 * rows, LANES), F32)],
        [gate, *near],
        [ANY] + [VMEM] * zs,
    )
    state_other = plan.swap(state_send, group=1)
    send_rows = 8 + 3 * EDGE
    sum_mine, send = call(
        functools.partial(total_kernel, plan),
        [part_shape, struct((send_rows, LANES), F32)],
        [low, low_other, high, high_other, state_mine],
    )

    wide_rows = send_rows + zs * (rows + scale_rows(slots))
    norm, relay, wide = call(
        functools.partial(core_kernel, plan),
        [struct((n, LANES), F32) for n in (8, send_rows, wide_rows)],
        [send, plan.swap(send, core=1), sum_mine, state_mine],
    )
    wide = plan.swap(wide, group=1)
    norms = [norm, wide] + [plan.swap(relay if k % 2 else norm, group=k) for k in range(2, groups)]

    fixes = call(fix_kernel, struct((8, LANES), F32), [step.reshape(1, 1), relay], [VMEM, ANY])

    total_params = own_len * plan.devices
    own = struct((rows, LANES), F32)
    table = struct((1, slots), F32)
    ins = [*norms, sum_mine, state_mine, state_other, fixes]
    new_master, weights, update, mn, vn, mt, vt = call(
        functools.partial(main_kernel, plan, total_params),
        [own, struct((plan.reps * rows, LANES), BF16), own, own, own, table, table],
        ins,
        scratch=[pltpu.VMEM(shape, F32), pltpu.VMEM(shape, F32), pltpu.VMEM((2, 2, EDGE, LANES), F32)],
    )
    return (
        new_master.reshape(-1),
        weights.reshape(-1),
        update.reshape(-1),
        mn.reshape(-1),
        vn.reshape(-1),
        mt.reshape(-1),
        vt.reshape(-1),
    )


def solution(mesh):
    own = P(ALL)
    in_specs = (P("shard", "rep", None), own, own, own, own, own, P())
    out_specs = (own, P("shard"), own, own, own, own, own)
    return jax.shard_map(on_device, mesh=mesh, in_specs=in_specs, out_specs=out_specs, check_vma=False)
```

```python
import functools

import jax
import jax.numpy as jnp
from jax import lax
from jax.experimental import pallas as pl
from jax.experimental.pallas import tpu as pltpu
from jax.sharding import PartitionSpec as P

BLOCK = 2048
LANES = 128
EDGE = BLOCK // 2 // LANES
ALL = ("shard", "rep")
BF16 = jnp.bfloat16
F32 = jnp.float32
VMEM = pl.BlockSpec(memory_space=pltpu.VMEM)
SMEM = pl.BlockSpec(memory_space=pltpu.SMEM)
ANY = pl.BlockSpec(memory_space=pl.ANY)
HBM = pl.BlockSpec(memory_space=pltpu.HBM)


class Plan:
    def __init__(self, own_len):
        self.shards = lax.axis_size("shard")
        self.reps = lax.axis_size("rep")
        self.devices = self.shards * self.reps
        self.xs = self.shards // 2
        self.zs = self.reps // 2
        self.groups = self.xs * 2
        self.rows = own_len // LANES

    def swap(self, value, core=0, z=0, group=0):
        x, y = group >> 1, group & 1
        mask = ((x << 1) | core) * self.reps + ((z << 1) | y)
        return lax.ppermute(value, ALL, [(i, i ^ mask) for i in range(self.devices)])


def place():
    shard, rep = lax.axis_index("shard"), lax.axis_index("rep")
    return shard // 2, shard % 2, rep // 2, rep % 2


def tree(values):
    values = list(values)
    while len(values) > 1:
        values = [a + b for a, b in zip(values[::2], values[1::2])]
    return values[0]


def call(kernel, outs, ins, in_specs=None, out_specs=None, scratch=(), limit=16):
    limit = int(limit * 1024 * 1024)
    return pl.pallas_call(
        kernel,
        out_shape=outs,
        in_specs=in_specs or [VMEM] * len(ins),
        out_specs=out_specs or jax.tree.map(lambda _: VMEM, outs),
        scratch_shapes=list(scratch),
        compiler_params=pltpu.CompilerParams(vmem_limit_bytes=limit),
    )(*ins)


def half_kernel(flip, count, length, x_ref, o_ref, buf, sem):
    _, core, _, _ = place()
    want = (core + flip) % 2
    rows = length // LANES
    copies = []
    for k in range(count):
        start = pl.multiple_of((2 * k + want) * length, length)
        copies.append(pltpu.make_async_copy(x_ref.at[:, pl.ds(start, length)], buf.at[k], sem.at[k]))
        copies[-1].start()
    for k in range(count):
        copies[k].wait()
        o_ref[pl.ds(k * rows, rows), :] = buf[k].astype(F32).reshape(rows, LANES).astype(BF16)


def half_call(plan, kernel, outs, ins):
    length = plan.reps * plan.rows * LANES
    return call(
        kernel,
        [jax.ShapeDtypeStruct((plan.xs * length // LANES, LANES), BF16), *outs],
        ins,
        in_specs=[ANY] * len(ins),
        scratch=[
            pltpu.VMEM((plan.xs, 1, length), BF16),
            pltpu.SemaphoreType.DMA((plan.xs,)),
            *(pltpu.VMEM(x.shape, x.dtype) for x in ins[1:]),
            *([pltpu.SemaphoreType.DMA((len(ins) - 1,))] if ins[1:] else []),
        ],
        limit=53.25,
    )


def own_kernel(plan, x_ref, o_ref, buf, sem):
    half_kernel(0, plan.xs, plan.reps * plan.rows * LANES, x_ref, o_ref, buf, sem)


def other_kernel(plan, x_ref, o_ref, buf, sem):
    half_kernel(1, plan.xs, plan.reps * plan.rows * LANES, x_ref, o_ref, buf, sem)


def pair_kernel(plan, mine_ref, other_ref, *outs):
    x, _, _, y = place()
    for k, out in enumerate(outs):
        to_x, to_y = x ^ (k >> 1), y ^ (k & 1)
        for z in range(plan.zs):
            start = pl.multiple_of((to_x * plan.reps + 2 * z + to_y) * plan.rows, plan.rows)
            rows = pl.ds(start, plan.rows)
            out[pl.ds(z * plan.rows, plan.rows), :] = mine_ref[rows, :].astype(F32) + other_ref[rows, :].astype(F32)


def part_kernel(*refs):
    *terms, low_ref, high_ref = refs
    half = low_ref.shape[0]
    low_ref[...] = tree([r[:half, :] for r in terms])
    high_ref[...] = tree([r[half:, :] for r in terms])


def add_kernel(mine_ref, other_ref, _, o_ref):
    o_ref[...] = mine_ref[...] + other_ref[...]


def state_rows(plan, slots):
    return 2 * plan.rows + scale_rows(slots)


def scale_rows(slots):
    return -(-slots // 8) * 8


def power(base, count):
    value, square = jnp.ones(count.shape, F32), jnp.full(count.shape, base, F32)
    for bit in range(8):
        value = jnp.where((count >> bit) & 1 == 1, value * square, value)
        square = square * square
    return value


def state_kernel(plan, mc_ref, vc_ref, ms_ref, vs_ref, master_ref, _, o_ref):
    o_ref = o_ref.at[0]
    rows, slots = plan.rows, ms_ref.shape[1]
    o_ref[0:rows, :] = vc_ref[...].astype(F32) * 256.0 + (mc_ref[...].astype(F32) + 128.0)
    o_ref[rows : 2 * rows, :] = master_ref[...]
    lane = lax.broadcasted_iota(jnp.int32, (1, LANES), 1)
    for j in range(slots):
        scales = jnp.where(lane < LANES // 2, ms_ref[:, j : j + 1], vs_ref[:, j : j + 1])
        o_ref[2 * rows + j : 2 * rows + j + 1, :] = scales


def decayed(state, scales, low, high):
    slot = (low + EDGE) // (2 * EDGE)
    scale = scales[slot : slot + 1, :]
    pair = state[low:high, :]
    v_code = jnp.floor(pair * (1.0 / 256.0))
    m_code = pair - (v_code * 256.0 + 128.0)
    m_scale, v_scale = scale[:, 0:1] * (0.9 / 127.0), scale[:, LANES // 2 : LANES // 2 + 1] * (0.95 / 255.0)
    return m_code * m_scale, v_code * v_scale


def pieces(plan, slots):
    return [(max(0, (2 * j - 1) * EDGE), min(plan.rows, (2 * j + 1) * EDGE)) for j in range(slots)]


def order_kernel(plan, _, *refs):
    *states, o_ref, send_ref = refs
    _, _, z, _ = place()
    for k, ref in enumerate(states):
        o_ref[z ^ k] = ref[0]
        send_ref[z ^ k] = ref[0, : send_ref.shape[1], :]


def token_kernel(x_ref, *refs):
    refs[-1][...] = x_ref[0:8, :]


def fix_kernel(step_ref, _, o_ref):
    count = jnp.broadcast_to(step_ref[...], (1, LANES))
    for j, base in enumerate((0.9, 0.95)):
        o_ref[j : j + 1, :] = 1.0 / (1.0 - power(base, count))


def squares(values):
    return jnp.sum((values * values).reshape(-1, 8, LANES), axis=0)


def total_kernel(plan, *refs):
    low_ref, low_other, high_ref, high_other, state_ref, sum_ref, send_ref = refs
    _, _, _, y = place()
    half = low_ref.shape[0]
    low, high = low_ref[...] + low_other[...], high_ref[...] + high_other[...]
    sum_ref[:half, :] = low
    sum_ref[half:, :] = high
    send_ref[0:8, :] = squares(low) + squares(high)

    def edge(z, start):
        send_ref[8 : 8 + EDGE, :] = sum_ref[z * plan.rows + start : z * plan.rows + start + EDGE, :]
        state = state_ref.at[z]
        old = decayed(state, state.at[2 * plan.rows :], start, start + EDGE)
        for k in range(2):
            send_ref[8 + (k + 1) * EDGE : 8 + (k + 2) * EDGE, :] = old[k]

    @pl.when(y == 0)
    def _():
        edge(0, 0)

    @pl.when(y == 1)
    def _():
        edge(plan.zs - 1, plan.rows - EDGE)


def core_kernel(mine_ref, other_ref, sum_ref, norm_ref, relay_ref, wide_ref):
    norm = mine_ref[0:8, :] + other_ref[0:8, :]
    norm_ref[...] = norm
    size = relay_ref.shape[0]
    for ref in (relay_ref, wide_ref):
        ref[0:8, :] = norm
        ref[8:size, :] = other_ref[8:, :]
    wide_ref[size:, :] = sum_ref[...]


def main_kernel(plan, total_params, *refs):
    norms, refs = refs[: plan.groups], refs[plan.groups :]
    (sum_mine, state_mine, state_other, fix_ref) = refs[:4]
    (master_out, weights_out, update_out, mn_out, vn_out, mt_out, vt_out) = refs[4:11]
    m_buf, v_buf, far = refs[11:]
    sum_other = norms[1].at[pl.ds(8 + 3 * EDGE, plan.zs * plan.rows)]
    x, core, z, y = place()
    rows = plan.rows
    slots = mt_out.shape[1]
    norm_sq = jnp.sum(tree([r[0:8, :] for r in norms]), keepdims=True)
    clip = jnp.minimum(1.0, float(total_params) ** 0.5 / (jnp.sqrt(norm_sq) + 1e-06))
    def scales_mine(k):
        return state_mine.at[k, 2 * rows :]

    def scales_other(k):
        return state_other.at[k, 2 * rows :]

    first, second = fix_ref[0:1, :], fix_ref[1:2, :]

    def moments(grad, m_decayed, v_decayed):
        scaled = grad * clip
        return m_decayed + 0.1 * scaled, v_decayed + 0.05 * scaled * scaled

    def step(grads, state, scales, low, high):
        m, v = moments(grads[low:high, :], *decayed(state, scales, low, high))
        update = m * first / (jnp.sqrt(v * second) + 1e-08)
        master = state[rows + low : rows + high, :]
        return m, v, update, master * (1.0 - 0.0001 * 0.1) - 0.0001 * update

    for k in range(plan.zs):
        sides = ((sum_mine, state_mine, scales_mine), (sum_other, state_other, scales_other))
        for flip, (sums, states, scales) in enumerate(sides):
            start = pl.multiple_of((2 * k + (y ^ flip)) * rows, rows)
            grads = sums.at[pl.ds(k * rows, rows)]
            out = jnp.concatenate([step(grads, states.at[k], scales(k), *piece)[3] for piece in pieces(plan, slots)], axis=0)
            weights_out[pl.ds(start, rows), :] = out.astype(BF16)

    grads = sum_mine.at[pl.ds(pl.multiple_of(z * rows, rows), rows)]
    for low, high in pieces(plan, slots):
        m, v, update, master = step(grads, state_mine.at[z], scales_mine(z), low, high)
        update_out[low:high, :] = update
        master_out[low:high, :] = master
        m_buf[low:high, :] = m
        v_buf[low:high, :] = v

    far[...] = jnp.zeros_like(far)

    def near(side, at_z, start):
        grad = sum_other[pl.ds(pl.multiple_of(at_z * rows + start, EDGE), EDGE), :]
        em, ev = moments(grad, *decayed(state_other.at[at_z], scales_other(at_z), start, start + EDGE))
        far[side, 0], far[side, 1] = jnp.abs(em), jnp.abs(ev)

    def across(side, shard):
        for k in range(1, plan.groups, 2):
            @pl.when((shard >= 0) & (shard < plan.shards) & ((x ^ (k >> 1)) == shard // 2))
            def _():
                em, ev = moments(*(norms[k][8 + j * EDGE : 8 + (j + 1) * EDGE, :] for j in range(3)))
                far[side, 0], far[side, 1] = jnp.abs(em), jnp.abs(ev)

    shard = 2 * x + core

    @pl.when(y == 0)
    def _():
        near(1, z, 0)

        @pl.when(z > 0)
        def _():
            near(0, z - 1, rows - EDGE)

        @pl.when(z == 0)
        def _():
            across(0, shard - 1)

    @pl.when(y == 1)
    def _():
        near(0, z, rows - EDGE)

        @pl.when(z < plan.zs - 1)
        def _():
            near(1, z + 1, 0)

        @pl.when(z == plan.zs - 1)
        def _():
            across(1, shard + 1)

    lane = lax.broadcasted_iota(jnp.int32, (1, LANES), 1)
    for which, (buf, table, norm_out) in enumerate(((m_buf, mt_out, mn_out), (v_buf, vt_out, vn_out))):
        line = jnp.zeros((1, LANES), F32)
        for j, (low, high) in enumerate(pieces(plan, slots)):
            values = buf[low:high, :]
            top = jnp.max(jnp.abs(values).reshape(-1, 8, LANES), axis=0)
            if j == 0:
                top = jnp.maximum(top, far[0, which])
            if j == slots - 1:
                top = jnp.maximum(top, far[1, which])
            top = jnp.max(top, keepdims=True)
            line = jnp.where(lane == j, top, line)
            norm_out[low:high, :] = values / (top + 1e-06)
        table[...] = line[:, :slots]


def on_device(grads, momentum_codes, variance_codes, momentum_scale, variance_scale, master, step):
    own_len = master.shape[0]
    slots = momentum_scale.shape[0]
    plan = Plan(own_len)
    rows, zs, groups = plan.rows, plan.zs, plan.groups
    struct = jax.ShapeDtypeStruct

    shape = (rows, LANES)
    state_shape = (state_rows(plan, slots), LANES)
    part_shape = struct((zs * rows, LANES), F32)
    half_shape = struct((zs * rows // 2, LANES), F32)

    flat = grads.reshape(1, -1)
    (send,) = half_call(plan, functools.partial(other_kernel, plan), [], [flat])
    arrived = plan.swap(send, core=1)
    (mine,) = half_call(plan, functools.partial(own_kernel, plan), [], [flat])
    blocks = call(functools.partial(pair_kernel, plan), [part_shape] * groups, [mine, arrived])

    sums = [plan.swap(blocks[k], group=k) for k in range(1, groups)]

    low, high = call(part_kernel, [half_shape] * 2, [blocks[0], *sums])

    states = call(
        functools.partial(state_kernel, plan),
        struct((1, *state_shape), F32),
        [
            momentum_codes.reshape(shape),
            variance_codes.reshape(shape),
            momentum_scale.reshape(1, slots),
            variance_scale.reshape(1, slots),
            master.reshape(shape),
            blocks[0],
        ],
        [VMEM] * 5 + [ANY],
    )
    near = [states] + [plan.swap(states, z=k) for k in range(1, zs)]

    gate = low
    bits = (zs - 1).bit_length()
    for bit in range(bits):
        high_other = plan.swap(high, z=1 << (bits - 1 - bit))
        low_other = plan.swap(low, z=1 << bit)
        if bit < bits - 1:
            high = call(add_kernel, half_shape, [high, high_other, low], [VMEM, VMEM, ANY])
            low = call(add_kernel, half_shape, [low, low_other, high], [VMEM, VMEM, ANY])
    gate = call(token_kernel, struct((8, LANES), F32), [gate, *near[2:]], [VMEM] + [ANY] * (zs - 2))
    state_mine, state_send = call(
        functools.partial(order_kernel, plan),
        [struct((zs, *state_shape), F32), struct((zs, *state_shape), F32)],
        [gate, *near],
        [ANY] + [VMEM] * zs,
    )
    state_other = plan.swap(state_send, group=1)
    send_rows = 8 + 3 * EDGE
    sum_mine, send = call(
        functools.partial(total_kernel, plan),
        [part_shape, struct((send_rows, LANES), F32)],
        [low, low_other, high, high_other, state_mine],
    )

    wide_rows = send_rows + zs * rows
    norm, relay, wide = call(
        core_kernel,
        [struct((n, LANES), F32) for n in (8, send_rows, wide_rows)],
        [send, plan.swap(send, core=1), sum_mine],
    )
    wide = plan.swap(wide, group=1)
    norms = [norm, wide] + [plan.swap(relay if k % 2 else norm, group=k) for k in range(2, groups)]

    fixes = call(fix_kernel, struct((8, LANES), F32), [step.reshape(1, 1), relay], [VMEM, ANY])

    total_params = own_len * plan.devices
    own = struct((rows, LANES), F32)
    table = struct((1, slots), F32)
    ins = [*norms, sum_mine, state_mine, state_other, fixes]
    new_master, weights, update, mn, vn, mt, vt = call(
        functools.partial(main_kernel, plan, total_params),
        [own, struct((plan.reps * rows, LANES), BF16), own, own, own, table, table],
        ins,
        scratch=[pltpu.VMEM(shape, F32), pltpu.VMEM(shape, F32), pltpu.VMEM((2, 2, EDGE, LANES), F32)],
    )
    return (
        new_master.reshape(-1),
        weights.reshape(-1),
        update.reshape(-1),
        mn.reshape(-1),
        vn.reshape(-1),
        mt.reshape(-1),
        vt.reshape(-1),
    )


def solution(mesh):
    own = P(ALL)
    in_specs = (P("shard", "rep", None), own, own, own, own, own, P())
    out_specs = (own, P("shard"), own, own, own, own, own)
    return jax.shard_map(on_device, mesh=mesh, in_specs=in_specs, out_specs=out_specs, check_vma=False)
```

```python
import functools

import jax
import jax.numpy as jnp
from jax import lax
from jax.experimental import pallas as pl
from jax.experimental.pallas import tpu as pltpu
from jax.sharding import PartitionSpec as P

BLOCK = 2048
LANES = 128
EDGE = BLOCK // 2 // LANES
ALL = ("shard", "rep")
BF16 = jnp.bfloat16
F32 = jnp.float32
VMEM = pl.BlockSpec(memory_space=pltpu.VMEM)
SMEM = pl.BlockSpec(memory_space=pltpu.SMEM)
ANY = pl.BlockSpec(memory_space=pl.ANY)
HBM = pl.BlockSpec(memory_space=pltpu.HBM)


class Plan:
    def __init__(self, own_len):
        self.shards = lax.axis_size("shard")
        self.reps = lax.axis_size("rep")
        self.devices = self.shards * self.reps
        self.xs = self.shards // 2
        self.zs = self.reps // 2
        self.groups = self.xs * 2
        self.rows = own_len // LANES

    def swap(self, value, core=0, z=0, group=0):
        x, y = group >> 1, group & 1
        mask = ((x << 1) | core) * self.reps + ((z << 1) | y)
        return lax.ppermute(value, ALL, [(i, i ^ mask) for i in range(self.devices)])


def place():
    shard, rep = lax.axis_index("shard"), lax.axis_index("rep")
    return shard // 2, shard % 2, rep // 2, rep % 2


def tree(values):
    values = list(values)
    while len(values) > 1:
        values = [a + b for a, b in zip(values[::2], values[1::2])]
    return values[0]


def call(kernel, outs, ins, in_specs=None, out_specs=None, scratch=(), limit=16):
    limit = int(limit * 1024 * 1024)
    return pl.pallas_call(
        kernel,
        out_shape=outs,
        in_specs=in_specs or [VMEM] * len(ins),
        out_specs=out_specs or jax.tree.map(lambda _: VMEM, outs),
        scratch_shapes=list(scratch),
        compiler_params=pltpu.CompilerParams(vmem_limit_bytes=limit),
    )(*ins)


def half_kernel(flip, count, length, x_ref, o_ref, buf, sem):
    _, core, _, _ = place()
    want = (core + flip) % 2
    rows = length // LANES
    copies = []
    for k in range(count):
        start = pl.multiple_of((2 * k + want) * length, length)
        copies.append(pltpu.make_async_copy(x_ref.at[:, pl.ds(start, length)], buf.at[k], sem.at[k]))
        copies[-1].start()
    for k in range(count):
        copies[k].wait()
        o_ref[pl.ds(k * rows, rows), :] = buf[k].astype(F32).reshape(rows, LANES).astype(BF16)


def half_call(plan, kernel, outs, ins):
    length = plan.reps * plan.rows * LANES
    return call(
        kernel,
        [jax.ShapeDtypeStruct((plan.xs * length // LANES, LANES), BF16), *outs],
        ins,
        in_specs=[ANY] * len(ins),
        scratch=[
            pltpu.VMEM((plan.xs, 1, length), BF16),
            pltpu.SemaphoreType.DMA((plan.xs,)),
            *(pltpu.VMEM(x.shape, x.dtype) for x in ins[1:]),
            *([pltpu.SemaphoreType.DMA((len(ins) - 1,))] if ins[1:] else []),
        ],
        limit=53.25,
    )


def own_kernel(plan, x_ref, o_ref, buf, sem):
    half_kernel(0, plan.xs, plan.reps * plan.rows * LANES, x_ref, o_ref, buf, sem)


def other_kernel(plan, x_ref, o_ref, buf, sem):
    half_kernel(1, plan.xs, plan.reps * plan.rows * LANES, x_ref, o_ref, buf, sem)


def pair_kernel(plan, mine_ref, other_ref, *outs):
    x, _, _, y = place()
    for k, out in enumerate(outs):
        to_x, to_y = x ^ (k >> 1), y ^ (k & 1)
        for z in range(plan.zs):
            start = pl.multiple_of((to_x * plan.reps + 2 * z + to_y) * plan.rows, plan.rows)
            rows = pl.ds(start, plan.rows)
            out[pl.ds(z * plan.rows, plan.rows), :] = mine_ref[rows, :].astype(F32) + other_ref[rows, :].astype(F32)


def part_kernel(*refs):
    *terms, low_ref, high_ref = refs
    half = low_ref.shape[0]
    low_ref[...] = tree([r[:half, :] for r in terms])
    high_ref[...] = tree([r[half:, :] for r in terms])


def add_kernel(mine_ref, other_ref, _, o_ref):
    o_ref[...] = mine_ref[...] + other_ref[...]


def state_rows(plan, slots):
    return 2 * plan.rows + scale_rows(slots)


def scale_rows(slots):
    return -(-slots // 8) * 8


def power(base, count):
    value, square = jnp.ones(count.shape, F32), jnp.full(count.shape, base, F32)
    for bit in range(8):
        value = jnp.where((count >> bit) & 1 == 1, value * square, value)
        square = square * square
    return value


def state_kernel(plan, mc_ref, vc_ref, ms_ref, vs_ref, master_ref, _, o_ref):
    o_ref = o_ref.at[0]
    rows, slots = plan.rows, ms_ref.shape[1]
    o_ref[0:rows, :] = vc_ref[...].astype(F32) * 256.0 + (mc_ref[...].astype(F32) + 128.0)
    o_ref[rows : 2 * rows, :] = master_ref[...]
    lane = lax.broadcasted_iota(jnp.int32, (1, LANES), 1)
    for j in range(slots):
        scales = jnp.where(lane < LANES // 2, ms_ref[:, j : j + 1], vs_ref[:, j : j + 1])
        o_ref[2 * rows + j : 2 * rows + j + 1, :] = scales


def decayed(state, scales, low, high):
    slot = (low + EDGE) // (2 * EDGE)
    return decode(state[low:high, :], scales[slot : slot + 1, :])


def decode(pair, scale):
    v_code = jnp.floor(pair * (1.0 / 256.0))
    m_code = pair - (v_code * 256.0 + 128.0)
    m_scale, v_scale = scale[:, 0:1] * (0.9 / 127.0), scale[:, LANES // 2 : LANES // 2 + 1] * (0.95 / 255.0)
    return m_code * m_scale, v_code * v_scale


def pieces(plan, slots):
    return [(max(0, (2 * j - 1) * EDGE), min(plan.rows, (2 * j + 1) * EDGE)) for j in range(slots)]


def order_kernel(plan, _, *refs):
    *states, o_ref, send_ref = refs
    _, _, z, _ = place()
    for k, ref in enumerate(states):
        o_ref[z ^ k] = ref[0]
        send_ref[z ^ k] = ref[0, : send_ref.shape[1], :]


def token_kernel(x_ref, *refs):
    refs[-1][...] = x_ref[0:8, :]


def fix_kernel(step_ref, _, o_ref):
    count = jnp.broadcast_to(step_ref[...], (1, LANES))
    for j, base in enumerate((0.9, 0.95)):
        o_ref[j : j + 1, :] = 1.0 / (1.0 - power(base, count))


def squares(values):
    return jnp.sum((values * values).reshape(-1, 8, LANES), axis=0)


def total_kernel(plan, *refs):
    low_ref, low_other, high_ref, high_other, state_ref, sum_ref, send_ref = refs
    _, _, _, y = place()
    half = low_ref.shape[0]
    low, high = low_ref[...] + low_other[...], high_ref[...] + high_other[...]
    sum_ref[:half, :] = low
    sum_ref[half:, :] = high
    send_ref[0:8, :] = squares(low) + squares(high)

    def edge(z, start):
        send_ref[8 : 8 + EDGE, :] = sum_ref[z * plan.rows + start : z * plan.rows + start + EDGE, :]
        state = state_ref.at[z]
        old = decayed(state, state.at[2 * plan.rows :], start, start + EDGE)
        for k in range(2):
            send_ref[8 + (k + 1) * EDGE : 8 + (k + 2) * EDGE, :] = old[k]

    @pl.when(y == 0)
    def _():
        edge(0, 0)

    @pl.when(y == 1)
    def _():
        edge(plan.zs - 1, plan.rows - EDGE)


def core_kernel(mine_ref, other_ref, sum_ref, norm_ref, relay_ref, wide_ref):
    norm = mine_ref[0:8, :] + other_ref[0:8, :]
    norm_ref[...] = norm
    size = relay_ref.shape[0]
    for ref in (relay_ref, wide_ref):
        ref[0:8, :] = norm
        ref[8:size, :] = other_ref[8:, :]
    wide_ref[size:, :] = sum_ref[...]


def main_kernel(plan, total_params, *refs):
    norms, refs = refs[: plan.groups], refs[plan.groups :]
    (sum_mine, state_mine, state_other, fix_ref) = refs[:4]
    (master_out, weights_out, update_out, mn_out, vn_out, mt_out, vt_out) = refs[4:11]
    m_buf, v_buf = refs[11:]
    sum_other = norms[1].at[pl.ds(8 + 3 * EDGE, plan.zs * plan.rows)]
    x, core, z, y = place()
    rows = plan.rows
    slots = mt_out.shape[1]
    norm_sq = jnp.sum(tree([r[0:8, :] for r in norms]), keepdims=True)
    clip = jnp.minimum(1.0, float(total_params) ** 0.5 / (jnp.sqrt(norm_sq) + 1e-06))
    def scales_mine(k):
        return state_mine.at[k, 2 * rows :]

    def scales_other(k):
        return state_other.at[k, 2 * rows :]

    first, second = fix_ref[0:1, :], fix_ref[1:2, :]

    def moments(grad, m_decayed, v_decayed):
        scaled = grad * clip
        return m_decayed + 0.1 * scaled, v_decayed + 0.05 * scaled * scaled

    def step(grads, state, scales, low, high):
        m, v = moments(grads[low:high, :], *decayed(state, scales, low, high))
        update = m * first / (jnp.sqrt(v * second) + 1e-08)
        master = state[rows + low : rows + high, :]
        return m, v, update, master * (1.0 - 0.0001 * 0.1) - 0.0001 * update

    for k in range(plan.zs):
        sides = ((sum_mine, state_mine, scales_mine), (sum_other, state_other, scales_other))
        for flip, (sums, states, scales) in enumerate(sides):
            start = pl.multiple_of((2 * k + (y ^ flip)) * rows, rows)
            grads = sums.at[pl.ds(k * rows, rows)]
            out = jnp.concatenate([step(grads, states.at[k], scales(k), *piece)[3] for piece in pieces(plan, slots)], axis=0)
            weights_out[pl.ds(start, rows), :] = out.astype(BF16)

    grads = sum_mine.at[pl.ds(pl.multiple_of(z * rows, rows), rows)]
    for low, high in pieces(plan, slots):
        m, v, update, master = step(grads, state_mine.at[z], scales_mine(z), low, high)
        update_out[low:high, :] = update
        master_out[low:high, :] = master
        m_buf[low:high, :] = m
        v_buf[low:high, :] = v

    def near(at_z, last):
        start = pl.multiple_of(last * (rows - EDGE), EDGE)
        grad = sum_other[pl.ds(pl.multiple_of(at_z * rows + start, EDGE), EDGE), :]
        pair = state_other[at_z, pl.ds(start, EDGE), :]
        scale = state_other[at_z, pl.ds(2 * rows + last * (slots - 1), 1), :]
        return grad, *decode(pair, scale)

    beside = [jnp.abs(value) for value in moments(*near(z, y))]
    next_z, shard = z - 1 + 2 * y, 2 * x + core - 1 + 2 * y
    inside = (next_z >= 0) & (next_z < plan.zs)
    terms = near(jnp.clip(next_z, 0, plan.zs - 1), 1 - y)
    for k in range(1, plan.groups, 2):
        here = jnp.logical_not(inside) & ((x ^ (k >> 1)) == shard // 2)
        terms = [jnp.where(here, norms[k][8 + j * EDGE : 8 + (j + 1) * EDGE, :], term) for j, term in enumerate(terms)]
    exists = inside | ((shard >= 0) & (shard < plan.shards))
    beyond = [jnp.where(exists, jnp.abs(value), 0.0) for value in moments(*terms)]
    first_far = [jnp.where(y == 0, p, q) for p, q in zip(beyond, beside)]
    last_far = [jnp.where(y == 0, q, p) for p, q in zip(beyond, beside)]

    lane = lax.broadcasted_iota(jnp.int32, (1, LANES), 1)
    for which, (buf, table, norm_out) in enumerate(((m_buf, mt_out, mn_out), (v_buf, vt_out, vn_out))):
        line = jnp.zeros((1, LANES), F32)
        for j, (low, high) in enumerate(pieces(plan, slots)):
            values = buf[low:high, :]
            top = jnp.max(jnp.abs(values).reshape(-1, 8, LANES), axis=0)
            if j == 0:
                top = jnp.maximum(top, first_far[which])
            if j == slots - 1:
                top = jnp.maximum(top, last_far[which])
            top = jnp.max(top, keepdims=True)
            line = jnp.where(lane == j, top, line)
            norm_out[low:high, :] = values / (top + 1e-06)
        table[...] = line[:, :slots]


def on_device(grads, momentum_codes, variance_codes, momentum_scale, variance_scale, master, step):
    own_len = master.shape[0]
    slots = momentum_scale.shape[0]
    plan = Plan(own_len)
    rows, zs, groups = plan.rows, plan.zs, plan.groups
    struct = jax.ShapeDtypeStruct

    shape = (rows, LANES)
    state_shape = (state_rows(plan, slots), LANES)
    part_shape = struct((zs * rows, LANES), F32)
    half_shape = struct((zs * rows // 2, LANES), F32)

    flat = grads.reshape(1, -1)
    (send,) = half_call(plan, functools.partial(other_kernel, plan), [], [flat])
    arrived = plan.swap(send, core=1)
    (mine,) = half_call(plan, functools.partial(own_kernel, plan), [], [flat])
    blocks = call(functools.partial(pair_kernel, plan), [part_shape] * groups, [mine, arrived])

    sums = [plan.swap(blocks[k], group=k) for k in range(1, groups)]

    low, high = call(part_kernel, [half_shape] * 2, [blocks[0], *sums])

    states = call(
        functools.partial(state_kernel, plan),
        struct((1, *state_shape), F32),
        [
            momentum_codes.reshape(shape),
            variance_codes.reshape(shape),
            momentum_scale.reshape(1, slots),
            variance_scale.reshape(1, slots),
            master.reshape(shape),
            blocks[0],
        ],
        [VMEM] * 5 + [ANY],
    )
    near = [states] + [plan.swap(states, z=k) for k in range(1, zs)]

    gate = low
    bits = (zs - 1).bit_length()
    for bit in range(bits):
        high_other = plan.swap(high, z=1 << (bits - 1 - bit))
        low_other = plan.swap(low, z=1 << bit)
        if bit < bits - 1:
            high = call(add_kernel, half_shape, [high, high_other, low], [VMEM, VMEM, ANY])
            low = call(add_kernel, half_shape, [low, low_other, high], [VMEM, VMEM, ANY])
    gate = call(token_kernel, struct((8, LANES), F32), [gate, *near[2:]], [VMEM] + [ANY] * (zs - 2))
    state_mine, state_send = call(
        functools.partial(order_kernel, plan),
        [struct((zs, *state_shape), F32), struct((zs, *state_shape), F32)],
        [gate, *near],
        [ANY] + [VMEM] * zs,
    )
    state_other = plan.swap(state_send, group=1)
    send_rows = 8 + 3 * EDGE
    sum_mine, send = call(
        functools.partial(total_kernel, plan),
        [part_shape, struct((send_rows, LANES), F32)],
        [low, low_other, high, high_other, state_mine],
    )

    wide_rows = send_rows + zs * rows
    norm, relay, wide = call(
        core_kernel,
        [struct((n, LANES), F32) for n in (8, send_rows, wide_rows)],
        [send, plan.swap(send, core=1), sum_mine],
    )
    wide = plan.swap(wide, group=1)
    norms = [norm, wide] + [plan.swap(relay if k % 2 else norm, group=k) for k in range(2, groups)]

    fixes = call(fix_kernel, struct((8, LANES), F32), [step.reshape(1, 1), relay], [VMEM, ANY])

    total_params = own_len * plan.devices
    own = struct((rows, LANES), F32)
    table = struct((1, slots), F32)
    ins = [*norms, sum_mine, state_mine, state_other, fixes]
    new_master, weights, update, mn, vn, mt, vt = call(
        functools.partial(main_kernel, plan, total_params),
        [own, struct((plan.reps * rows, LANES), BF16), own, own, own, table, table],
        ins,
        scratch=[pltpu.VMEM(shape, F32), pltpu.VMEM(shape, F32)],
    )
    return (
        new_master.reshape(-1),
        weights.reshape(-1),
        update.reshape(-1),
        mn.reshape(-1),
        vn.reshape(-1),
        mt.reshape(-1),
        vt.reshape(-1),
    )


def solution(mesh):
    own = P(ALL)
    in_specs = (P("shard", "rep", None), own, own, own, own, own, P())
    out_specs = (own, P("shard"), own, own, own, own, own)
    return jax.shard_map(on_device, mesh=mesh, in_specs=in_specs, out_specs=out_specs, check_vma=False)
```

```python
import functools

import jax
import jax.numpy as jnp
from jax import lax
from jax.experimental import pallas as pl
from jax.experimental.pallas import tpu as pltpu
from jax.sharding import PartitionSpec as P

BLOCK = 2048
LANES = 128
EDGE = BLOCK // 2 // LANES
ALL = ("shard", "rep")
BF16 = jnp.bfloat16
F32 = jnp.float32
VMEM = pl.BlockSpec(memory_space=pltpu.VMEM)
SMEM = pl.BlockSpec(memory_space=pltpu.SMEM)
ANY = pl.BlockSpec(memory_space=pl.ANY)
HBM = pl.BlockSpec(memory_space=pltpu.HBM)


class Plan:
    def __init__(self, own_len):
        self.shards = lax.axis_size("shard")
        self.reps = lax.axis_size("rep")
        self.devices = self.shards * self.reps
        self.xs = self.shards // 2
        self.zs = self.reps // 2
        self.groups = self.xs * 2
        self.rows = own_len // LANES

    def swap(self, value, core=0, z=0, group=0):
        x, y = group >> 1, group & 1
        mask = ((x << 1) | core) * self.reps + ((z << 1) | y)
        return lax.ppermute(value, ALL, [(i, i ^ mask) for i in range(self.devices)])


def place():
    shard, rep = lax.axis_index("shard"), lax.axis_index("rep")
    return shard // 2, shard % 2, rep // 2, rep % 2


def tree(values):
    values = list(values)
    while len(values) > 1:
        values = [a + b for a, b in zip(values[::2], values[1::2])]
    return values[0]


def call(kernel, outs, ins, in_specs=None, out_specs=None, scratch=(), limit=16):
    limit = int(limit * 1024 * 1024)
    return pl.pallas_call(
        kernel,
        out_shape=outs,
        in_specs=in_specs or [VMEM] * len(ins),
        out_specs=out_specs or jax.tree.map(lambda _: VMEM, outs),
        scratch_shapes=list(scratch),
        compiler_params=pltpu.CompilerParams(vmem_limit_bytes=limit),
    )(*ins)


def half_kernel(flip, count, length, x_ref, o_ref, buf, sem):
    _, core, _, _ = place()
    want = (core + flip) % 2
    rows = length // LANES
    copies = []
    for k in range(count):
        start = pl.multiple_of((2 * k + want) * length, length)
        copies.append(pltpu.make_async_copy(x_ref.at[:, pl.ds(start, length)], buf.at[k], sem.at[k]))
        copies[-1].start()
    for k in range(count):
        copies[k].wait()
        o_ref[pl.ds(k * rows, rows), :] = buf[k].astype(F32).reshape(rows, LANES).astype(BF16)


def half_call(plan, kernel, outs, ins):
    length = plan.reps * plan.rows * LANES
    return call(
        kernel,
        [jax.ShapeDtypeStruct((plan.xs * length // LANES, LANES), BF16), *outs],
        ins,
        in_specs=[ANY] * len(ins),
        scratch=[
            pltpu.VMEM((plan.xs, 1, length), BF16),
            pltpu.SemaphoreType.DMA((plan.xs,)),
            *(pltpu.VMEM(x.shape, x.dtype) for x in ins[1:]),
            *([pltpu.SemaphoreType.DMA((len(ins) - 1,))] if ins[1:] else []),
        ],
        limit=53.25,
    )


def own_kernel(plan, x_ref, o_ref, buf, sem):
    half_kernel(0, plan.xs, plan.reps * plan.rows * LANES, x_ref, o_ref, buf, sem)


def other_kernel(plan, x_ref, o_ref, buf, sem):
    half_kernel(1, plan.xs, plan.reps * plan.rows * LANES, x_ref, o_ref, buf, sem)


def pair_kernel(plan, mine_ref, other_ref, *outs):
    x, _, _, y = place()
    for k, out in enumerate(outs):
        to_x, to_y = x ^ (k >> 1), y ^ (k & 1)
        for z in range(plan.zs):
            start = pl.multiple_of((to_x * plan.reps + 2 * z + to_y) * plan.rows, plan.rows)
            rows = pl.ds(start, plan.rows)
            out[pl.ds(z * plan.rows, plan.rows), :] = mine_ref[rows, :].astype(F32) + other_ref[rows, :].astype(F32)


def part_kernel(*refs):
    *terms, low_ref, high_ref = refs
    half = low_ref.shape[0]
    low_ref[...] = tree([r[:half, :] for r in terms])
    high_ref[...] = tree([r[half:, :] for r in terms])


def add_kernel(mine_ref, other_ref, _, o_ref):
    o_ref[...] = mine_ref[...] + other_ref[...]


def state_rows(plan, slots):
    return 2 * plan.rows + scale_rows(slots)


def scale_rows(slots):
    return -(-slots // 8) * 8


def power(base, count):
    value, square = jnp.ones(count.shape, F32), jnp.full(count.shape, base, F32)
    for bit in range(8):
        value = jnp.where((count >> bit) & 1 == 1, value * square, value)
        square = square * square
    return value


def state_kernel(plan, mc_ref, vc_ref, ms_ref, vs_ref, master_ref, _, o_ref):
    o_ref = o_ref.at[0]
    rows, slots = plan.rows, ms_ref.shape[1]
    o_ref[0:rows, :] = vc_ref[...].astype(F32) * 256.0 + (mc_ref[...].astype(F32) + 128.0)
    o_ref[rows : 2 * rows, :] = master_ref[...]
    lane = lax.broadcasted_iota(jnp.int32, (1, LANES), 1)
    for j in range(slots):
        scales = jnp.where(lane < LANES // 2, ms_ref[:, j : j + 1], vs_ref[:, j : j + 1])
        o_ref[2 * rows + j : 2 * rows + j + 1, :] = scales


def decayed(state, scales, low, high):
    slot = (low + EDGE) // (2 * EDGE)
    return decode(state[low:high, :], scales[slot : slot + 1, :])


def decode(pair, scale):
    v_code = jnp.floor(pair * (1.0 / 256.0))
    m_code = pair - (v_code * 256.0 + 128.0)
    m_scale, v_scale = scale[:, 0:1] * (0.9 / 127.0), scale[:, LANES // 2 : LANES // 2 + 1] * (0.95 / 255.0)
    return m_code * m_scale, v_code * v_scale


def pieces(plan, slots):
    return [(max(0, (2 * j - 1) * EDGE), min(plan.rows, (2 * j + 1) * EDGE)) for j in range(slots)]


def order_kernel(plan, _, *refs):
    *states, o_ref, send_ref = refs
    _, _, z, _ = place()
    for k, ref in enumerate(states):
        o_ref[z ^ k] = ref[0]
        send_ref[z ^ k] = ref[0, : send_ref.shape[1], :]


def token_kernel(x_ref, *refs):
    refs[-1][...] = x_ref[0:8, :]


def fix_kernel(step_ref, _, o_ref):
    count = jnp.broadcast_to(step_ref[...], (1, LANES))
    for j, base in enumerate((0.9, 0.95)):
        o_ref[j : j + 1, :] = 1.0 / (1.0 - power(base, count))


def squares(values):
    return jnp.sum((values * values).reshape(-1, 8, LANES), axis=0)


def total_kernel(plan, slots, *refs):
    low_ref, low_other, high_ref, high_other, state_ref, sum_ref, send_ref = refs
    _, _, _, y = place()
    half = low_ref.shape[0]
    low, high = low_ref[...] + low_other[...], high_ref[...] + high_other[...]
    sum_ref[:half, :] = low
    sum_ref[half:, :] = high
    send_ref[0:8, :] = squares(low) + squares(high)

    at_z, start = y * (plan.zs - 1), pl.multiple_of(y * (plan.rows - EDGE), EDGE)
    pair = state_ref[at_z, pl.ds(start, EDGE), :]
    scale = state_ref[at_z, pl.ds(2 * plan.rows + y * (slots - 1), 1), :]
    edge = sum_ref[pl.ds(pl.multiple_of(at_z * plan.rows + start, EDGE), EDGE), :]
    for k, value in enumerate((edge, *decode(pair, scale))):
        send_ref[8 + k * EDGE : 8 + (k + 1) * EDGE, :] = value


def core_kernel(mine_ref, other_ref, sum_ref, norm_ref, relay_ref, wide_ref):
    norm = mine_ref[0:8, :] + other_ref[0:8, :]
    norm_ref[...] = norm
    size = relay_ref.shape[0]
    for ref in (relay_ref, wide_ref):
        ref[0:8, :] = norm
        ref[8:size, :] = other_ref[8:, :]
    wide_ref[size:, :] = sum_ref[...]


def main_kernel(plan, total_params, *refs):
    norms, refs = refs[: plan.groups], refs[plan.groups :]
    (sum_mine, state_mine, state_other, fix_ref) = refs[:4]
    (master_out, weights_out, update_out, mn_out, vn_out, mt_out, vt_out) = refs[4:11]
    m_buf, v_buf = refs[11:]
    sum_other = norms[1].at[pl.ds(8 + 3 * EDGE, plan.zs * plan.rows)]
    x, core, z, y = place()
    rows = plan.rows
    slots = mt_out.shape[1]
    norm_sq = jnp.sum(tree([r[0:8, :] for r in norms]), keepdims=True)
    clip = jnp.minimum(1.0, float(total_params) ** 0.5 / (jnp.sqrt(norm_sq) + 1e-06))
    def scales_mine(k):
        return state_mine.at[k, 2 * rows :]

    def scales_other(k):
        return state_other.at[k, 2 * rows :]

    first, second = fix_ref[0:1, :], fix_ref[1:2, :]

    def moments(grad, m_decayed, v_decayed):
        scaled = grad * clip
        return m_decayed + 0.1 * scaled, v_decayed + 0.05 * scaled * scaled

    def step(grads, state, scales, low, high):
        m, v = moments(grads[low:high, :], *decayed(state, scales, low, high))
        update = m * first / (jnp.sqrt(v * second) + 1e-08)
        master = state[rows + low : rows + high, :]
        return m, v, update, master * (1.0 - 0.0001 * 0.1) - 0.0001 * update

    for k in range(plan.zs):
        sides = ((sum_mine, state_mine, scales_mine), (sum_other, state_other, scales_other))
        for flip, (sums, states, scales) in enumerate(sides):
            start = pl.multiple_of((2 * k + (y ^ flip)) * rows, rows)
            grads = sums.at[pl.ds(k * rows, rows)]
            out = jnp.concatenate([step(grads, states.at[k], scales(k), *piece)[3] for piece in pieces(plan, slots)], axis=0)
            weights_out[pl.ds(start, rows), :] = out.astype(BF16)

    grads = sum_mine.at[pl.ds(pl.multiple_of(z * rows, rows), rows)]
    for low, high in pieces(plan, slots):
        m, v, update, master = step(grads, state_mine.at[z], scales_mine(z), low, high)
        update_out[low:high, :] = update
        master_out[low:high, :] = master
        m_buf[low:high, :] = m
        v_buf[low:high, :] = v

    def near(at_z, last):
        start = pl.multiple_of(last * (rows - EDGE), EDGE)
        grad = sum_other[pl.ds(pl.multiple_of(at_z * rows + start, EDGE), EDGE), :]
        pair = state_other[at_z, pl.ds(start, EDGE), :]
        scale = state_other[at_z, pl.ds(2 * rows + last * (slots - 1), 1), :]
        return grad, *decode(pair, scale)

    beside = [jnp.abs(value) for value in moments(*near(z, y))]
    next_z, shard = z - 1 + 2 * y, 2 * x + core - 1 + 2 * y
    inside = (next_z >= 0) & (next_z < plan.zs)
    terms = near(jnp.clip(next_z, 0, plan.zs - 1), 1 - y)
    for k in range(1, plan.groups, 2):
        here = jnp.logical_not(inside) & ((x ^ (k >> 1)) == shard // 2)
        terms = [jnp.where(here, norms[k][8 + j * EDGE : 8 + (j + 1) * EDGE, :], term) for j, term in enumerate(terms)]
    exists = inside | ((shard >= 0) & (shard < plan.shards))
    beyond = [jnp.where(exists, jnp.abs(value), 0.0) for value in moments(*terms)]
    first_far = [jnp.where(y == 0, p, q) for p, q in zip(beyond, beside)]
    last_far = [jnp.where(y == 0, q, p) for p, q in zip(beyond, beside)]

    lane = lax.broadcasted_iota(jnp.int32, (1, LANES), 1)
    for which, (buf, table, norm_out) in enumerate(((m_buf, mt_out, mn_out), (v_buf, vt_out, vn_out))):
        line = jnp.zeros((1, LANES), F32)
        for j, (low, high) in enumerate(pieces(plan, slots)):
            values = buf[low:high, :]
            top = jnp.max(jnp.abs(values).reshape(-1, 8, LANES), axis=0)
            if j == 0:
                top = jnp.maximum(top, first_far[which])
            if j == slots - 1:
                top = jnp.maximum(top, last_far[which])
            top = jnp.max(top, keepdims=True)
            line = jnp.where(lane == j, top, line)
            norm_out[low:high, :] = values / (top + 1e-06)
        table[...] = line[:, :slots]


def on_device(grads, momentum_codes, variance_codes, momentum_scale, variance_scale, master, step):
    own_len = master.shape[0]
    slots = momentum_scale.shape[0]
    plan = Plan(own_len)
    rows, zs, groups = plan.rows, plan.zs, plan.groups
    struct = jax.ShapeDtypeStruct

    shape = (rows, LANES)
    state_shape = (state_rows(plan, slots), LANES)
    part_shape = struct((zs * rows, LANES), F32)
    half_shape = struct((zs * rows // 2, LANES), F32)

    flat = grads.reshape(1, -1)
    (send,) = half_call(plan, functools.partial(other_kernel, plan), [], [flat])
    arrived = plan.swap(send, core=1)
    (mine,) = half_call(plan, functools.partial(own_kernel, plan), [], [flat])
    blocks = call(functools.partial(pair_kernel, plan), [part_shape] * groups, [mine, arrived])

    sums = [plan.swap(blocks[k], group=k) for k in range(1, groups)]

    low, high = call(part_kernel, [half_shape] * 2, [blocks[0], *sums])

    states = call(
        functools.partial(state_kernel, plan),
        struct((1, *state_shape), F32),
        [
            momentum_codes.reshape(shape),
            variance_codes.reshape(shape),
            momentum_scale.reshape(1, slots),
            variance_scale.reshape(1, slots),
            master.reshape(shape),
            blocks[0],
        ],
        [VMEM] * 5 + [ANY],
    )
    near = [states] + [plan.swap(states, z=k) for k in range(1, zs)]

    gate = low
    bits = (zs - 1).bit_length()
    for bit in range(bits):
        high_other = plan.swap(high, z=1 << (bits - 1 - bit))
        low_other = plan.swap(low, z=1 << bit)
        if bit < bits - 1:
            high = call(add_kernel, half_shape, [high, high_other, low], [VMEM, VMEM, ANY])
            low = call(add_kernel, half_shape, [low, low_other, high], [VMEM, VMEM, ANY])
    gate = call(token_kernel, struct((8, LANES), F32), [gate, *near[3:]], [VMEM] + [ANY] * (zs - 3))
    state_mine, state_send = call(
        functools.partial(order_kernel, plan),
        [struct((zs, *state_shape), F32), struct((zs, *state_shape), F32)],
        [gate, *near],
        [ANY] + [VMEM] * zs,
    )
    state_other = plan.swap(state_send, group=1)
    send_rows = 8 + 3 * EDGE
    sum_mine, send = call(
        functools.partial(total_kernel, plan, slots),
        [part_shape, struct((send_rows, LANES), F32)],
        [low, low_other, high, high_other, state_mine],
    )

    wide_rows = send_rows + zs * rows
    norm, relay, wide = call(
        core_kernel,
        [struct((n, LANES), F32) for n in (8, send_rows, wide_rows)],
        [send, plan.swap(send, core=1), sum_mine],
    )
    wide = plan.swap(wide, group=1)
    norms = [norm, wide] + [plan.swap(relay if k % 2 else norm, group=k) for k in range(2, groups)]

    fixes = call(fix_kernel, struct((8, LANES), F32), [step.reshape(1, 1), relay], [VMEM, ANY])

    total_params = own_len * plan.devices
    own = struct((rows, LANES), F32)
    table = struct((1, slots), F32)
    ins = [*norms, sum_mine, state_mine, state_other, fixes]
    new_master, weights, update, mn, vn, mt, vt = call(
        functools.partial(main_kernel, plan, total_params),
        [own, struct((plan.reps * rows, LANES), BF16), own, own, own, table, table],
        ins,
        scratch=[pltpu.VMEM(shape, F32), pltpu.VMEM(shape, F32)],
    )
    return (
        new_master.reshape(-1),
        weights.reshape(-1),
        update.reshape(-1),
        mn.reshape(-1),
        vn.reshape(-1),
        mt.reshape(-1),
        vt.reshape(-1),
    )


def solution(mesh):
    own = P(ALL)
    in_specs = (P("shard", "rep", None), own, own, own, own, own, P())
    out_specs = (own, P("shard"), own, own, own, own, own)
    return jax.shard_map(on_device, mesh=mesh, in_specs=in_specs, out_specs=out_specs, check_vma=False)
```

```python
import functools

import jax
import jax.numpy as jnp
from jax import lax
from jax.experimental import pallas as pl
from jax.experimental.pallas import tpu as pltpu
from jax.sharding import PartitionSpec as P

BLOCK = 2048
LANES = 128
EDGE = BLOCK // 2 // LANES
ALL = ("shard", "rep")
BF16 = jnp.bfloat16
F32 = jnp.float32
VMEM = pl.BlockSpec(memory_space=pltpu.VMEM)
SMEM = pl.BlockSpec(memory_space=pltpu.SMEM)
ANY = pl.BlockSpec(memory_space=pl.ANY)
HBM = pl.BlockSpec(memory_space=pltpu.HBM)


class Plan:
    def __init__(self, own_len):
        self.shards = lax.axis_size("shard")
        self.reps = lax.axis_size("rep")
        self.devices = self.shards * self.reps
        self.xs = self.shards // 2
        self.zs = self.reps // 2
        self.groups = self.xs * 2
        self.rows = own_len // LANES

    def swap(self, value, core=0, z=0, group=0):
        x, y = group >> 1, group & 1
        mask = ((x << 1) | core) * self.reps + ((z << 1) | y)
        return lax.ppermute(value, ALL, [(i, i ^ mask) for i in range(self.devices)])


def place():
    shard, rep = lax.axis_index("shard"), lax.axis_index("rep")
    return shard // 2, shard % 2, rep // 2, rep % 2


def tree(values):
    values = list(values)
    while len(values) > 1:
        values = [a + b for a, b in zip(values[::2], values[1::2])]
    return values[0]


def call(kernel, outs, ins, in_specs=None, out_specs=None, scratch=(), limit=16):
    limit = int(limit * 1024 * 1024)
    return pl.pallas_call(
        kernel,
        out_shape=outs,
        in_specs=in_specs or [VMEM] * len(ins),
        out_specs=out_specs or jax.tree.map(lambda _: VMEM, outs),
        scratch_shapes=list(scratch),
        compiler_params=pltpu.CompilerParams(vmem_limit_bytes=limit),
    )(*ins)


def half_kernel(flip, count, length, x_ref, o_ref, buf, sem):
    _, core, _, _ = place()
    want = (core + flip) % 2
    rows = length // LANES
    copies = []
    for k in range(count):
        start = pl.multiple_of((2 * k + want) * length, length)
        copies.append(pltpu.make_async_copy(x_ref.at[:, pl.ds(start, length)], buf.at[k], sem.at[k]))
        copies[-1].start()
    for k in range(count):
        copies[k].wait()
        o_ref[pl.ds(k * rows, rows), :] = buf[k].astype(F32).reshape(rows, LANES).astype(BF16)


def half_call(plan, kernel, outs, ins):
    length = plan.reps * plan.rows * LANES
    return call(
        kernel,
        [jax.ShapeDtypeStruct((plan.xs * length // LANES, LANES), BF16), *outs],
        ins,
        in_specs=[ANY] * len(ins),
        scratch=[
            pltpu.VMEM((plan.xs, 1, length), BF16),
            pltpu.SemaphoreType.DMA((plan.xs,)),
            *(pltpu.VMEM(x.shape, x.dtype) for x in ins[1:]),
            *([pltpu.SemaphoreType.DMA((len(ins) - 1,))] if ins[1:] else []),
        ],
        limit=53.25,
    )


def own_kernel(plan, x_ref, o_ref, buf, sem):
    half_kernel(0, plan.xs, plan.reps * plan.rows * LANES, x_ref, o_ref, buf, sem)


def other_kernel(plan, x_ref, o_ref, buf, sem):
    half_kernel(1, plan.xs, plan.reps * plan.rows * LANES, x_ref, o_ref, buf, sem)


def pair_kernel(plan, mine_ref, other_ref, *outs):
    x, _, _, y = place()
    for k, out in enumerate(outs):
        to_x, to_y = x ^ (k >> 1), y ^ (k & 1)
        for z in range(plan.zs):
            start = pl.multiple_of((to_x * plan.reps + 2 * z + to_y) * plan.rows, plan.rows)
            rows = pl.ds(start, plan.rows)
            out[pl.ds(z * plan.rows, plan.rows), :] = mine_ref[rows, :].astype(F32) + other_ref[rows, :].astype(F32)


def part_kernel(*refs):
    *terms, low_ref, high_ref = refs
    half = low_ref.shape[0]
    low_ref[...] = tree([r[:half, :] for r in terms])
    high_ref[...] = tree([r[half:, :] for r in terms])


def add_kernel(mine_ref, other_ref, _, o_ref):
    o_ref[...] = mine_ref[...] + other_ref[...]


def state_rows(plan, slots):
    return 2 * plan.rows + scale_rows(slots)


def scale_rows(slots):
    return -(-slots // 8) * 8


def power(base, count):
    value, square = jnp.ones(count.shape, F32), jnp.full(count.shape, base, F32)
    for bit in range(8):
        value = jnp.where((count >> bit) & 1 == 1, value * square, value)
        square = square * square
    return value


def state_kernel(plan, mc_ref, vc_ref, ms_ref, vs_ref, master_ref, _, o_ref):
    o_ref = o_ref.at[0]
    rows, slots = plan.rows, ms_ref.shape[1]
    o_ref[0:rows, :] = vc_ref[...].astype(F32) * 256.0 + (mc_ref[...].astype(F32) + 128.0)
    o_ref[rows : 2 * rows, :] = master_ref[...]
    lane = lax.broadcasted_iota(jnp.int32, (1, LANES), 1)
    for j in range(slots):
        scales = jnp.where(lane < LANES // 2, ms_ref[:, j : j + 1], vs_ref[:, j : j + 1])
        o_ref[2 * rows + j : 2 * rows + j + 1, :] = scales


def decayed(state, scales, low, high):
    slot = (low + EDGE) // (2 * EDGE)
    return decode(state[low:high, :], scales[slot : slot + 1, :])


def codes(pair):
    v_code = jnp.floor(pair * (1.0 / 256.0))
    return pair - (v_code * 256.0 + 128.0), v_code


def factors(scale):
    return scale[:, 0:1] * (0.9 / 127.0), scale[:, LANES // 2 : LANES // 2 + 1] * (0.95 / 255.0)


def decode(pair, scale):
    (m_code, v_code), (m_scale, v_scale) = codes(pair), factors(scale)
    return m_code * m_scale, v_code * v_scale


def pieces(plan, slots):
    return [(max(0, (2 * j - 1) * EDGE), min(plan.rows, (2 * j + 1) * EDGE)) for j in range(slots)]


def order_kernel(plan, _, *refs):
    *states, o_ref, send_ref = refs
    _, _, z, _ = place()
    for k, ref in enumerate(states):
        o_ref[z ^ k] = ref[0]
        send_ref[z ^ k] = ref[0, : send_ref.shape[1], :]


def token_kernel(x_ref, *refs):
    refs[-1][...] = x_ref[0:8, :]


def fix_kernel(step_ref, _, o_ref):
    count = jnp.broadcast_to(step_ref[...], (1, LANES))
    for j, base in enumerate((0.9, 0.95)):
        o_ref[j : j + 1, :] = 1.0 / (1.0 - power(base, count))


def squares(values):
    return jnp.sum((values * values).reshape(-1, 8, LANES), axis=0)


def total_kernel(plan, *refs):
    low_ref, low_other, high_ref, high_other, state_ref, sum_ref, send_ref = refs
    _, _, _, y = place()
    half = low_ref.shape[0]
    low, high = low_ref[...] + low_other[...], high_ref[...] + high_other[...]
    sum_ref[:half, :] = low
    sum_ref[half:, :] = high
    send_ref[0:8, :] = squares(low) + squares(high)

    def edge(z, start):
        send_ref[8 : 8 + EDGE, :] = sum_ref[z * plan.rows + start : z * plan.rows + start + EDGE, :]
        state = state_ref.at[z]
        old = decayed(state, state.at[2 * plan.rows :], start, start + EDGE)
        for k in range(2):
            send_ref[8 + (k + 1) * EDGE : 8 + (k + 2) * EDGE, :] = old[k]

    @pl.when(y == 0)
    def _():
        edge(0, 0)

    @pl.when(y == 1)
    def _():
        edge(plan.zs - 1, plan.rows - EDGE)


def core_kernel(mine_ref, other_ref, sum_ref, norm_ref, relay_ref, wide_ref):
    norm = mine_ref[0:8, :] + other_ref[0:8, :]
    norm_ref[...] = norm
    size = relay_ref.shape[0]
    for ref in (relay_ref, wide_ref):
        ref[0:8, :] = norm
        ref[8:size, :] = other_ref[8:, :]
    wide_ref[size:, :] = sum_ref[...]


def main_kernel(plan, total_params, *refs):
    norms, refs = refs[: plan.groups], refs[plan.groups :]
    (sum_mine, state_mine, state_other, fix_ref) = refs[:4]
    (master_out, weights_out, update_out, mn_out, vn_out, mt_out, vt_out) = refs[4:11]
    m_buf, v_buf = refs[11:]
    sum_other = norms[1].at[pl.ds(8 + 3 * EDGE, plan.zs * plan.rows)]
    x, core, z, y = place()
    rows = plan.rows
    slots = mt_out.shape[1]
    norm_sq = jnp.sum(tree([r[0:8, :] for r in norms]), keepdims=True)
    clip = jnp.minimum(1.0, float(total_params) ** 0.5 / (jnp.sqrt(norm_sq) + 1e-06))
    def scales_mine(k):
        return state_mine.at[k, 2 * rows :]

    def scales_other(k):
        return state_other.at[k, 2 * rows :]

    first, second = fix_ref[0:1, :], fix_ref[1:2, :]

    def moments(grad, m_decayed, v_decayed):
        scaled = grad * clip
        return m_decayed + 0.1 * scaled, v_decayed + 0.05 * scaled * scaled

    def step(grads, state, scales, low, high):
        m, v = moments(grads[low:high, :], *decayed(state, scales, low, high))
        update = m * first / (jnp.sqrt(v * second) + 1e-08)
        master = state[rows + low : rows + high, :]
        return m, v, update, master * (1.0 - 0.0001 * 0.1) - 0.0001 * update

    m_gain, v_gain = 0.1 * clip * first, 0.05 * clip * clip * second

    def weights(grads, state, scales, low, high):
        slot = (low + EDGE) // (2 * EDGE)
        m_scale, v_scale = factors(scales[slot : slot + 1, :])
        (m_code, v_code), grad = codes(state[low:high, :]), grads[low:high, :]
        m, v = m_code * (m_scale * first) + grad * m_gain, v_code * (v_scale * second) + grad * grad * v_gain
        master = state[rows + low : rows + high, :]
        return master * (1.0 - 0.0001 * 0.1) - 0.0001 * (m / (jnp.sqrt(v) + 1e-08))

    for k in range(plan.zs):
        sides = ((sum_mine, state_mine, scales_mine), (sum_other, state_other, scales_other))
        for flip, (sums, states, scales) in enumerate(sides):
            start = pl.multiple_of((2 * k + (y ^ flip)) * rows, rows)
            grads = sums.at[pl.ds(k * rows, rows)]
            out = jnp.concatenate([weights(grads, states.at[k], scales(k), *piece) for piece in pieces(plan, slots)], axis=0)
            weights_out[pl.ds(start, rows), :] = out.astype(BF16)

    grads = sum_mine.at[pl.ds(pl.multiple_of(z * rows, rows), rows)]
    for low, high in pieces(plan, slots):
        m, v, update, master = step(grads, state_mine.at[z], scales_mine(z), low, high)
        update_out[low:high, :] = update
        master_out[low:high, :] = master
        m_buf[low:high, :] = m
        v_buf[low:high, :] = v

    def near(at_z, last):
        start = pl.multiple_of(last * (rows - EDGE), EDGE)
        grad = sum_other[pl.ds(pl.multiple_of(at_z * rows + start, EDGE), EDGE), :]
        pair = state_other[at_z, pl.ds(start, EDGE), :]
        scale = state_other[at_z, pl.ds(2 * rows + last * (slots - 1), 1), :]
        return grad, *decode(pair, scale)

    beside = [jnp.abs(value) for value in moments(*near(z, y))]
    next_z, shard = z - 1 + 2 * y, 2 * x + core - 1 + 2 * y
    inside = (next_z >= 0) & (next_z < plan.zs)
    terms = near(jnp.clip(next_z, 0, plan.zs - 1), 1 - y)
    for k in range(1, plan.groups, 2):
        here = jnp.logical_not(inside) & ((x ^ (k >> 1)) == shard // 2)
        terms = [jnp.where(here, norms[k][8 + j * EDGE : 8 + (j + 1) * EDGE, :], term) for j, term in enumerate(terms)]
    exists = inside | ((shard >= 0) & (shard < plan.shards))
    beyond = [jnp.where(exists, jnp.abs(value), 0.0) for value in moments(*terms)]
    first_far = [jnp.where(y == 0, p, q) for p, q in zip(beyond, beside)]
    last_far = [jnp.where(y == 0, q, p) for p, q in zip(beyond, beside)]

    lane = lax.broadcasted_iota(jnp.int32, (1, LANES), 1)
    for which, (buf, table, norm_out) in enumerate(((m_buf, mt_out, mn_out), (v_buf, vt_out, vn_out))):
        line = jnp.zeros((1, LANES), F32)
        for j, (low, high) in enumerate(pieces(plan, slots)):
            values = buf[low:high, :]
            top = jnp.max(jnp.abs(values).reshape(-1, 8, LANES), axis=0)
            if j == 0:
                top = jnp.maximum(top, first_far[which])
            if j == slots - 1:
                top = jnp.maximum(top, last_far[which])
            top = jnp.max(top, keepdims=True)
            line = jnp.where(lane == j, top, line)
            norm_out[low:high, :] = values / (top + 1e-06)
        table[...] = line[:, :slots]


def on_device(grads, momentum_codes, variance_codes, momentum_scale, variance_scale, master, step):
    own_len = master.shape[0]
    slots = momentum_scale.shape[0]
    plan = Plan(own_len)
    rows, zs, groups = plan.rows, plan.zs, plan.groups
    struct = jax.ShapeDtypeStruct

    shape = (rows, LANES)
    state_shape = (state_rows(plan, slots), LANES)
    part_shape = struct((zs * rows, LANES), F32)
    half_shape = struct((zs * rows // 2, LANES), F32)

    flat = grads.reshape(1, -1)
    (send,) = half_call(plan, functools.partial(other_kernel, plan), [], [flat])
    arrived = plan.swap(send, core=1)
    (mine,) = half_call(plan, functools.partial(own_kernel, plan), [], [flat])
    blocks = call(functools.partial(pair_kernel, plan), [part_shape] * groups, [mine, arrived])

    sums = [plan.swap(blocks[k], group=k) for k in range(1, groups)]

    low, high = call(part_kernel, [half_shape] * 2, [blocks[0], *sums])

    states = call(
        functools.partial(state_kernel, plan),
        struct((1, *state_shape), F32),
        [
            momentum_codes.reshape(shape),
            variance_codes.reshape(shape),
            momentum_scale.reshape(1, slots),
            variance_scale.reshape(1, slots),
            master.reshape(shape),
            blocks[0],
        ],
        [VMEM] * 5 + [ANY],
    )
    near = [states] + [plan.swap(states, z=k) for k in range(1, zs)]

    gate = low
    bits = (zs - 1).bit_length()
    for bit in range(bits):
        high_other = plan.swap(high, z=1 << (bits - 1 - bit))
        low_other = plan.swap(low, z=1 << bit)
        if bit < bits - 1:
            high = call(add_kernel, half_shape, [high, high_other, low], [VMEM, VMEM, ANY])
            low = call(add_kernel, half_shape, [low, low_other, high], [VMEM, VMEM, ANY])
    gate = call(token_kernel, struct((8, LANES), F32), [gate, *near[2:]], [VMEM] + [ANY] * (zs - 2))
    state_mine, state_send = call(
        functools.partial(order_kernel, plan),
        [struct((zs, *state_shape), F32), struct((zs, *state_shape), F32)],
        [gate, *near],
        [ANY] + [VMEM] * zs,
    )
    state_other = plan.swap(state_send, group=1)
    send_rows = 8 + 3 * EDGE
    sum_mine, send = call(
        functools.partial(total_kernel, plan),
        [part_shape, struct((send_rows, LANES), F32)],
        [low, low_other, high, high_other, state_mine],
    )

    wide_rows = send_rows + zs * rows
    norm, relay, wide = call(
        core_kernel,
        [struct((n, LANES), F32) for n in (8, send_rows, wide_rows)],
        [send, plan.swap(send, core=1), sum_mine],
    )
    wide = plan.swap(wide, group=1)
    norms = [norm, wide] + [plan.swap(relay if k % 2 else norm, group=k) for k in range(2, groups)]

    fixes = call(fix_kernel, struct((8, LANES), F32), [step.reshape(1, 1), relay], [VMEM, ANY])

    total_params = own_len * plan.devices
    own = struct((rows, LANES), F32)
    table = struct((1, slots), F32)
    ins = [*norms, sum_mine, state_mine, state_other, fixes]
    new_master, weights, update, mn, vn, mt, vt = call(
        functools.partial(main_kernel, plan, total_params),
        [own, struct((plan.reps * rows, LANES), BF16), own, own, own, table, table],
        ins,
        scratch=[pltpu.VMEM(shape, F32), pltpu.VMEM(shape, F32)],
    )
    return (
        new_master.reshape(-1),
        weights.reshape(-1),
        update.reshape(-1),
        mn.reshape(-1),
        vn.reshape(-1),
        mt.reshape(-1),
        vt.reshape(-1),
    )


def solution(mesh):
    own = P(ALL)
    in_specs = (P("shard", "rep", None), own, own, own, own, own, P())
    out_specs = (own, P("shard"), own, own, own, own, own)
    return jax.shard_map(on_device, mesh=mesh, in_specs=in_specs, out_specs=out_specs, check_vma=False)
```
